32 devices in a mesh: pb: 4 (over y, x), ka: 8 (over z, core).
Axes of the slice: x: 2, y: 2, z: 4, core: 2. Of those that a mesh axis runs over, the one named last changes fastest.
Arguments:
- tokens: bfloat16 [2048, 7168], P('ka', 'pb'), may hold values from -6 to 6
- kv_weight: bfloat16 [7168, 576], P('pb'), may hold values from -0.0625 to 0.0625
- queries: bfloat16 [2048, 36864], P('pb', 'ka'), may hold values from -384 to 384
- block_list: int32 [16, 16], P('pb'), may hold values from -1 to 15, as said below
Outputs:
- attended: bfloat16 [2048, 32768], P('pb', 'ka')
The draws below stay inside these ranges and needn't reach their ends.
Inputs may be any that keep to these rules, and one draw needn't show every extreme that they name: `block_list`: row i lists distinct key blocks j <= i in ascending order, followed by -1 in its unused slots; every row lists block 0; the row of the last block fills all 16 slots. The rows of one aligned group of 4 query blocks list at most 2 distinct blocks of one aligned group of 2 key blocks, and 2 is reached in every draw.
All inputs are finite; a program needn't handle non-finite values.
Results may differ from the reference program's by a relative error of at most 0.012.
Values may be sent and summed in bfloat16 or wider, within the bound.
No kernel may reach another device: no remote copies, remote signals or barrier semaphores. Data moves between devices by JAX's collectives and lax.ppermute only.
A program may use at most 128 MiB of HBM per device.

```python
import math
import jax
import jax.numpy as jnp
from jax import lax

D = 7168
H = 64
KVL = 512
RD = 64
QK = 192
BLK = 128
MAXSEL = 16
KB = 2
NB = 16
QB = 4
CAP = 2
S = 2048
N_KA = 8


def draw_queries(key, part):
    values = jax.random.normal(jax.random.fold_in(key, 21), (S, H * (KVL + RD)), jnp.float32)
    values = jnp.clip(values, -6.0, 6.0)
    return values.astype(jnp.bfloat16)


def draw_block_list(key, part):
    set_scores = jax.random.randint(jax.random.fold_in(key, 31), (NB // QB, N_KA, KB), 0, 1 << 20)
    within = jnp.arange(KB, dtype=jnp.int32)
    set_scores = set_scores * KB + within
    anchor = (jnp.arange(N_KA, dtype=jnp.int32)[:, None] == 0) & (within[None, :] == 0)
    set_scores = jnp.where(anchor[None], jnp.int32(1 << 30), set_scores)
    beaten = jnp.sum((set_scores[..., None, :] > set_scores[..., :, None]).astype(jnp.int32), axis=-1)
    membership_flag = (beaten < CAP).reshape(NB // QB, NB)
    query_ids = jnp.arange(NB, dtype=jnp.int32)
    member_rows = membership_flag[query_ids // QB]
    candidate = member_rows & (query_ids[None, :] <= query_ids[:, None])
    priority = jax.random.randint(jax.random.fold_in(key, 32), (NB, NB), 0, 1 << 16) * NB + query_ids[None, :]
    last_row = query_ids[:, None] == NB - 1
    first_run = query_ids[None, :] < KB
    priority = priority + jnp.where(last_row & first_run, 1 << 29, 0) + jnp.where(query_ids[None, :] == 0, 1 << 30, 0)
    priority = jnp.where(candidate, priority, -1)
    ranked_blocks, picked = lax.top_k(priority, MAXSEL)
    wanted = jax.random.randint(jax.random.fold_in(key, 33), (NB, 1), 1, MAXSEL + 1)
    wanted = jnp.where(last_row, MAXSEL, wanted)
    valid = (ranked_blocks >= 0) & (jnp.arange(MAXSEL, dtype=jnp.int32)[None, :] < wanted)
    ordered = jnp.sort(jnp.where(valid, picked.astype(jnp.int32), NB), axis=1)
    return jnp.where(ordered == NB, -1, ordered).astype(jnp.int32)


def levels(key, extent, split, smallest, largest):
    def one(position, shards_of):
        steps = jax.random.uniform(jax.random.fold_in(jax.random.fold_in(key, 6), position), (shards_of,), jnp.float32, smallest / len(split), largest / len(split))
        return jnp.repeat(jnp.exp(steps), extent[position] // shards_of).reshape((-1,) + (1,) * (len(extent) - position - 1))

    level = one(*split[0])
    for cut in split[1:]:
        level = level * one(*cut)
    return level


def bell_draw(rng, shape, scale, bound, shards=(), held_as=jnp.bfloat16):
    level = levels(rng, shape, shards, -0.22, 0.18) if shards else 1.0
    drawn = jax.random.normal(rng, shape, jnp.float32) * scale * level
    return jnp.minimum(jnp.maximum(drawn, -bound), bound).astype(held_as)


def setup_inputs(seed: int = 0) -> dict:
    keys = jax.random.split(jax.random.key(seed), 5)
    return {
        "tokens": bell_draw(keys[0], (S, D), 1.0, 6.0, ((0, 8), (1, 4))),
        "kv_weight": bell_draw(keys[1], (D, KVL + RD), D ** -0.5, 0.0625, ((0, 4),)),
        "queries": draw_queries(jax.random.fold_in(keys[4], 71), 0),
        "block_list": draw_block_list(jax.random.fold_in(keys[4], 71), 0),
    }


def scale_rows(matrix):
    return matrix * lax.rsqrt(lax.optimization_barrier(jnp.mean(matrix * matrix, axis=-1, keepdims=True)) + 1e-06)

def rotate_cols(rotary, positions):
    half = rotary.shape[1] // 2
    steps = jnp.arange(half, dtype=jnp.float32)
    freq = jnp.exp(steps * (-2.0 * math.log(10000.0) / rotary.shape[1]))
    angle = positions.astype(jnp.float32)[:, None] * freq[None, :]
    cosine = jnp.cos(angle)
    sine = jnp.sin(angle)
    first = rotary[:, :half]
    second = rotary[:, half:]
    return jnp.concatenate([first * cosine - second * sine, second * cosine + first * sine], axis=1)

def reference(tokens, kv_weight, queries, block_list):
    width = KVL + RD
    projected = jnp.dot(tokens, kv_weight, preferred_element_type=jnp.float32)
    latent = scale_rows(projected[:, :KVL])
    rotary = rotate_cols(projected[:, KVL:], jnp.arange(S, dtype=jnp.int32))
    key_rows = jnp.concatenate([latent, rotary], axis=1).astype(jnp.bfloat16)
    key_blocks = key_rows.reshape(NB, BLK, width)
    query_blocks = queries.reshape(NB, BLK, H, width)
    offsets = jnp.arange(BLK, dtype=jnp.int32)
    factor = 1.0 / math.sqrt(QK)

    def one_block(inputs):
        block_index, query_block, listed = inputs
        chosen = jnp.maximum(listed, 0).astype(jnp.int32)
        selected_keys = key_blocks[chosen].reshape(MAXSEL * BLK, width).astype(jnp.float32)
        selected_values = selected_keys[:, :KVL]
        scores = jnp.einsum('qhd,kd->hqk', query_block.astype(jnp.float32), selected_keys) * factor
        key_pos = (chosen[:, None] * BLK + offsets[None, :]).reshape(MAXSEL * BLK)
        slot_live = jnp.broadcast_to((listed >= 0)[:, None], (MAXSEL, BLK)).reshape(MAXSEL * BLK)
        query_pos = block_index * BLK + offsets
        permitted_mask = slot_live[None, :] & (key_pos[None, :] <= query_pos[:, None])
        scores = jnp.where(permitted_mask[None], scores, -jnp.inf)
        highest = lax.optimization_barrier(jnp.max(scores, axis=-1, keepdims=True))
        weights = jnp.exp(scores - highest)
        weight_brain_float = (weights / lax.optimization_barrier(jnp.sum(weights, axis=-1, keepdims=True))).astype(jnp.bfloat16)
        blended = jnp.einsum('hqk,kd->qhd', weight_brain_float.astype(jnp.float32), selected_values)
        return blended.reshape(BLK, H * KVL).astype(jnp.bfloat16)
    result = lax.map(one_block, (jnp.arange(NB, dtype=jnp.int32), query_blocks, block_list))
    return result.reshape(NB * BLK, H * KVL)
```

```python
import functools
import math

import jax
import jax.numpy as jnp
from jax import lax
from jax.experimental import pallas as pl
from jax.experimental.pallas import tpu as pltpu
from jax.sharding import PartitionSpec as P

KVL = 512
RD = 64
QK = 192
BLK = 128
LANES = 128
WIDTH = KVL + RD
PADDED = KVL + 2 * RD
SCALE = math.log2(math.e) / math.sqrt(QK)


def packed_rows(rows):
    return rows * 4 + (rows // 2 if rows % 32 == 0 else rows)


def swap(x, axis_name, offset, count):
    return lax.ppermute(x, axis_name, [(i, i ^ offset) for i in range(count)])


def project_kernel(tokens_ref, weight_ref, *rest):
    outs, (tok, wgt, total, sem) = rest[:-4], rest[-4:]
    steps = tok.shape[0]
    depth = tok.shape[2]
    copies = []
    for t in range(steps):
        a = pltpu.make_async_copy(tokens_ref.at[:, pl.ds(t * depth, depth)], tok.at[t], sem.at[0, t])
        b = pltpu.make_async_copy(weight_ref.at[pl.ds(t * depth, depth), :], wgt.at[t], sem.at[1, t])
        a.start()
        b.start()
        copies.append((a, b))
    acc = None
    for t in range(steps):
        copies[t][0].wait()
        copies[t][1].wait()
        part = jnp.dot(tok[t], wgt[t], preferred_element_type=jnp.float32)
        acc = part if acc is None else acc + part
    total[...] = acc
    rows = outs[0].shape[0]
    me = lax.axis_index("pb")
    for k, out in enumerate(outs):
        out[...] = total[pl.ds(pl.multiple_of((me ^ k) * rows, rows), rows), :]


def project(tokens, kv_weight, parts):
    rows, features = tokens.shape
    depth = 256
    steps = features // depth
    return pl.pallas_call(
        project_kernel,
        out_shape=[jax.ShapeDtypeStruct((rows // parts, WIDTH), jnp.float32)] * parts,
        in_specs=[pl.BlockSpec(memory_space=pl.ANY)] * 2,
        out_specs=[pl.BlockSpec(memory_space=pltpu.VMEM)] * parts,
        scratch_shapes=[
            pltpu.VMEM((steps, rows, depth), jnp.bfloat16),
            pltpu.VMEM((steps, depth, WIDTH), jnp.bfloat16),
            pltpu.VMEM((rows, WIDTH), jnp.float32),
            pltpu.SemaphoreType.DMA((2, steps)),
        ],
        compiler_params=pltpu.CompilerParams(vmem_limit_bytes=24 * 2**20),
        name="project",
    )(tokens, kv_weight)


def finish_kernel(cos_ref, sin_ref, *rest):
    parts, out = rest[:-1], rest[-1]
    total = parts[0][...]
    for part in parts[1:]:
        total = total + part[...]
    rows = total.shape[0]
    latent = total[:, :KVL]
    latent = latent * lax.rsqrt(jnp.mean(latent * latent, axis=-1, keepdims=True) + 1e-06)
    for c in range(KVL // LANES):
        out[c * rows : (c + 1) * rows, :] = latent[:, c * LANES : (c + 1) * LANES].astype(jnp.bfloat16)
    rotary = total[:, KVL:]
    half = RD // 2
    turned = jnp.concatenate([rotary[:, half:], rotary[:, :half]], axis=1)
    rotary = rotary * cos_ref[...] + turned * sin_ref[...]
    if rows % 32 == 0:
        both = jnp.concatenate([rotary[: rows // 2], rotary[rows // 2 :]], axis=1)
    else:
        both = jnp.concatenate([rotary, jnp.zeros_like(rotary)], axis=1)
    out[4 * rows :, :] = both.astype(jnp.bfloat16)


def finish(parts, first_row):
    rows = parts[0].shape[0]
    half = RD // 2
    freq = jnp.exp(jnp.arange(half, dtype=jnp.float32) * (-2.0 * math.log(10000.0) / RD))
    position = (first_row + jnp.arange(rows, dtype=jnp.int32)).astype(jnp.float32)
    angle = position[:, None] * freq[None, :]
    cosine, sine = jnp.cos(angle), jnp.sin(angle)
    cosine = jnp.concatenate([cosine, cosine], axis=1)
    sine = jnp.concatenate([-sine, sine], axis=1)
    return pl.pallas_call(
        finish_kernel,
        out_shape=jax.ShapeDtypeStruct((packed_rows(rows), LANES), jnp.bfloat16),
        name="finish",
    )(cosine, sine, *parts)


def attend_kernel(layout, parts, chunk, list_ref, q_ref, *rest):
    count = len(layout)
    pieces = rest[:count]
    o_ref, buf, sem, kx, q2, s_ref, m_ref, l_ref, acc = rest[count:]
    group = pl.program_id(0)
    heads = q_ref.shape[1] // WIDTH
    rows = heads * BLK
    block = lax.axis_index("pb") * pl.num_programs(0) + group
    packed = packed_rows(chunk)

    @pl.when(group == 0)
    def _():
        copies = []
        at = 0
        for i, piece in enumerate(pieces):
            copies.append(pltpu.make_async_copy(piece, buf.at[pl.ds(at, piece.shape[0]), :], sem.at[i]))
            copies[-1].start()
            at += piece.shape[0]
        kx[:, KVL:] = jnp.zeros((kx.shape[0], LANES), jnp.bfloat16)
        pb, ka = lax.axis_index("pb"), lax.axis_index("ka")
        at = 0
        for i, offsets in enumerate(layout):
            copies[i].wait()
            for dk, dq in offsets:
                row = pl.multiple_of(((ka ^ dk) * parts + (pb ^ dq)) * chunk, chunk)
                for c in range(KVL // LANES):
                    kx[pl.ds(row, chunk), c * LANES : (c + 1) * LANES] = buf[at + c * chunk : at + (c + 1) * chunk, :]
                rotary = buf[at + 4 * chunk : at + packed, :]
                if chunk % 32 == 0:
                    kx[pl.ds(row, chunk // 2), KVL : KVL + RD] = rotary[:, :RD]
                    kx[pl.ds(row + chunk // 2, chunk // 2), KVL : KVL + RD] = rotary[:, RD:]
                else:
                    kx[pl.ds(row, chunk), KVL:] = rotary
                at += packed

    for h in range(heads):
        c = h * WIDTH
        if c % LANES:
            wide = q_ref[:, c - RD : c + WIDTH]
            wide = jnp.concatenate([wide[:, RD:], wide[:, :RD]], axis=1)
        elif c + PADDED <= q_ref.shape[1]:
            wide = q_ref[:, c : c + PADDED]
        else:
            wide = jnp.concatenate([q_ref[:, c : c + WIDTH], jnp.zeros((BLK, RD), jnp.bfloat16)], axis=1)
        q2[h * BLK : (h + 1) * BLK, :] = wide

    listed = jnp.int32(0)
    for t in range(list_ref.shape[1]):
        listed = listed + (list_ref[group, t] >= 0).astype(jnp.int32)
    pairs = (listed + 1) // 2
    m_ref[...] = jnp.full_like(m_ref, -jnp.inf)

    def slots(j):
        return jnp.maximum(list_ref[group, 2 * j], 0), jnp.maximum(list_ref[group, 2 * j + 1], 0)

    def key_rows(j, width):
        i0, i1 = slots(j)
        return jnp.concatenate(
            [
                kx[pl.ds(pl.multiple_of(i0 * BLK, BLK), BLK), :width],
                kx[pl.ds(pl.multiple_of(i1 * BLK, BLK), BLK), :width],
            ],
            axis=0,
        )

    def scores(j, masked):
        keys = key_rows(j, PADDED)
        step = min(512, rows)
        for t in range(rows // step):
            sl = slice(t * step, (t + 1) * step)
            s = lax.dot_general(q2[sl, :], keys, (((1,), (1,)), ((), ())), preferred_element_type=jnp.float32)
            if masked:
                i0, i1 = slots(j)
                i1 = jnp.where(list_ref[group, 2 * j + 1] >= 0, i1, 1 << 20)
                gap = lax.broadcasted_iota(jnp.int32, (BLK, BLK), 0) - lax.broadcasted_iota(jnp.int32, (BLK, BLK), 1)
                gap = gap + block * BLK
                bias = jnp.concatenate(
                    [jnp.where(gap >= i0 * BLK, 0.0, -jnp.inf), jnp.where(gap >= i1 * BLK, 0.0, -jnp.inf)], axis=1
                )
                s = (s.reshape(-1, BLK, 2 * BLK) + bias[None]).reshape(step, 2 * BLK)
            s_ref[j, sl, :] = s
            m_ref[sl, :] = jnp.maximum(m_ref[sl, :], jnp.maximum(s[:, :BLK], s[:, BLK:]))

    @pl.loop(0, pairs - 1)
    def _(j):
        scores(j, False)

    scores(pairs - 1, True)
    m_ref[...] = jnp.broadcast_to(jnp.max(m_ref[...], axis=1, keepdims=True) * SCALE, m_ref.shape)
    l_ref[...] = jnp.zeros_like(l_ref)
    acc[...] = jnp.zeros_like(acc)

    @pl.loop(0, pairs)
    def _(j):
        values = key_rows(j, KVL)
        step = min(256, rows)
        for t in range(rows // step):
            sl = slice(t * step, (t + 1) * step)
            highest = m_ref[sl, :]
            s = s_ref[j, sl, :]
            p0 = jnp.exp2(s[:, :BLK] * SCALE - highest)
            p1 = jnp.exp2(s[:, BLK:] * SCALE - highest)
            l_ref[sl, :] = l_ref[sl, :] + (p0 + p1)
            p = jnp.concatenate([p0.astype(jnp.bfloat16), p1.astype(jnp.bfloat16)], axis=1)
            acc[sl, :] = acc[sl, :] + jnp.dot(p, values, preferred_element_type=jnp.float32)

    for h in range(heads):
        sl = slice(h * BLK, (h + 1) * BLK)
        inverse = 1.0 / jnp.sum(l_ref[sl, :], axis=1, keepdims=True)
        o_ref[:, h * KVL : (h + 1) * KVL] = (acc[sl, :] * inverse).astype(jnp.bfloat16)


def attend(block_list, queries, pieces, layout, parts, chunk, key_count):
    groups = queries.shape[0] // BLK
    heads = queries.shape[1] // WIDTH
    rows = heads * BLK
    slots = block_list.shape[1]
    return pl.pallas_call(
        functools.partial(attend_kernel, layout, parts, chunk),
        grid_spec=pltpu.PrefetchScalarGridSpec(
            num_scalar_prefetch=1,
            grid=(groups,),
            in_specs=[pl.BlockSpec((BLK, queries.shape[1]), lambda g, _: (g, 0))]
            + [pl.BlockSpec(memory_space=pl.ANY)] * len(pieces),
            out_specs=pl.BlockSpec((BLK, heads * KVL), lambda g, _: (g, 0)),
            scratch_shapes=[
                pltpu.VMEM((sum(p.shape[0] for p in pieces), LANES), jnp.bfloat16),
                pltpu.SemaphoreType.DMA((len(pieces),)),
                pltpu.VMEM((key_count, PADDED), jnp.bfloat16),
                pltpu.VMEM((rows, PADDED), jnp.bfloat16),
                pltpu.VMEM((slots // 2, rows, 2 * BLK), jnp.float32),
                pltpu.VMEM((rows, LANES), jnp.float32),
                pltpu.VMEM((rows, LANES), jnp.float32),
                pltpu.VMEM((rows, KVL), jnp.float32),
            ],
        ),
        out_shape=jax.ShapeDtypeStruct((queries.shape[0], heads * KVL), jnp.bfloat16),
        compiler_params=pltpu.CompilerParams(vmem_limit_bytes=56 * 2**20),
        name="attend",
    )(block_list, queries, *pieces)


def per_device(n_pb, n_ka, tokens, kv_weight, queries, block_list):
    local_rows = tokens.shape[0]
    chunk = local_rows // n_pb
    partials = project(tokens, kv_weight, n_pb)
    arrived = [partials[0]] + [swap(partials[k], "pb", k, n_pb) for k in range(1, n_pb)]
    first_row = lax.axis_index("ka") * local_rows + lax.axis_index("pb") * chunk
    own = finish(arrived, first_row)

    far = range(2, n_ka, 2)
    ring = [0] + list(far)
    column = jnp.concatenate([own] + [swap(own, "ka", k, n_ka) for k in far], axis=0)
    sets = [(column, [(k, 0) for k in ring])]
    if n_pb == 4:
        corner = swap(own, "pb", 3, n_pb)
        for k in (1, 2):
            sets.append((swap(column, "pb", k, n_pb), [(d, k) for d in ring]))
        corners = jnp.concatenate([corner] + [swap(corner, "ka", k, n_ka) for k in far], axis=0)
        sets.append((corners, [(d, 3) for d in ring]))
    else:
        for k in range(1, n_pb):
            sets.append((swap(column, "pb", k, n_pb), [(d, k) for d in ring]))
    sets += [(swap(piece, "ka", 1, n_ka), [(d ^ 1, k) for d, k in offsets]) for piece, offsets in sets]
    pieces = [piece for piece, _ in sets]
    layout = [offsets for _, offsets in sets]
    return attend(block_list, queries, pieces, layout, n_pb, chunk, local_rows * n_ka)


def solution(mesh):
    in_specs = (P("ka", "pb"), P("pb", None), P("pb", "ka"), P("pb", None))
    out_specs = P("pb", "ka")
    return jax.shard_map(
        functools.partial(per_device, mesh.shape["pb"], mesh.shape["ka"]),
        mesh=mesh,
        in_specs=in_specs,
        out_specs=out_specs,
        check_vma=False,
    )
```

```python
import functools
import math

import jax
import jax.numpy as jnp
from jax import lax
from jax.experimental import pallas as pl
from jax.experimental.pallas import tpu as pltpu
from jax.sharding import PartitionSpec as P

KVL = 512
RD = 64
QK = 192
BLK = 128
LANES = 128
WIDTH = KVL + RD
PADDED = KVL + 2 * RD
MASKED = -1e30
LOWEST = -3e38
TILE = 1024
SCALE = math.log2(math.e) / math.sqrt(QK)


def packed_rows(rows):
    return rows * 4 + (rows // 2 if rows % 32 == 0 else rows)


def swap(x, axis_name, offset, count):
    return lax.ppermute(x, axis_name, [(i, i ^ offset) for i in range(count)])


def project_kernel(tokens_ref, weight_ref, *rest):
    outs, (tok, wgt, total, sem) = rest[:-4], rest[-4:]
    steps, _, depth = tok.shape
    copies = []
    for t in range(steps):
        cut = pl.ds(t * depth, depth)
        pair = [
            pltpu.make_async_copy(tokens_ref.at[:, cut], tok.at[t], sem.at[0, t]),
            pltpu.make_async_copy(weight_ref.at[:, cut], wgt.at[t], sem.at[1, t]),
        ]
        for copy in pair:
            copy.start()
        copies.append(pair)
    acc = None
    for t in range(steps):
        for copy in copies[t]:
            copy.wait()
        part = lax.dot_general(tok[t], wgt[t], (((1,), (1,)), ((), ())), preferred_element_type=jnp.float32)
        acc = part if acc is None else acc + part
    total[...] = acc
    rows = outs[0].shape[0]
    me = lax.axis_index("pb")
    for k, out in enumerate(outs):
        out[...] = total[pl.ds(pl.multiple_of((me ^ k) * rows, rows), rows), :]


def project(tokens, kv_weight, parts):
    rows, features = tokens.shape
    depth = 256
    steps = features // depth
    return pl.pallas_call(
        project_kernel,
        out_shape=[jax.ShapeDtypeStruct((rows // parts, WIDTH), jnp.float32)] * parts,
        in_specs=[pl.BlockSpec(memory_space=pltpu.HBM)] * 2,
        out_specs=[pl.BlockSpec(memory_space=pltpu.VMEM)] * parts,
        scratch_shapes=[
            pltpu.VMEM((steps, rows, depth), jnp.bfloat16),
            pltpu.VMEM((steps, WIDTH, depth), jnp.bfloat16),
            pltpu.VMEM((rows, WIDTH), jnp.float32),
            pltpu.SemaphoreType.DMA((2, steps)),
        ],
        compiler_params=pltpu.CompilerParams(vmem_limit_bytes=60 * 2**20),
        name="project",
    )(tokens, kv_weight.T)


def finish_kernel(cos_ref, sin_ref, *rest):
    parts, out = rest[:-1], rest[-1]
    total = parts[0][...]
    for part in parts[1:]:
        total = total + part[...]
    rows = total.shape[0]
    latent = total[:, :KVL]
    latent = latent * lax.rsqrt(jnp.mean(latent * latent, axis=-1, keepdims=True) + 1e-06)
    for c in range(KVL // LANES):
        out[c * rows : (c + 1) * rows, :] = latent[:, c * LANES : (c + 1) * LANES].astype(jnp.bfloat16)
    rotary = total[:, KVL:]
    half = RD // 2
    turned = jnp.concatenate([rotary[:, half:], rotary[:, :half]], axis=1)
    rotary = rotary * cos_ref[...] + turned * sin_ref[...]
    if rows % 32 == 0:
        both = jnp.concatenate([rotary[: rows // 2], rotary[rows // 2 :]], axis=1)
    else:
        both = jnp.concatenate([rotary, jnp.zeros_like(rotary)], axis=1)
    out[4 * rows :, :] = both.astype(jnp.bfloat16)


def finish(parts, first_row):
    rows = parts[0].shape[0]
    half = RD // 2
    freq = jnp.exp(jnp.arange(half, dtype=jnp.float32) * (-2.0 * math.log(10000.0) / RD))
    position = (first_row + jnp.arange(rows, dtype=jnp.int32)).astype(jnp.float32)
    angle = position[:, None] * freq[None, :]
    cosine, sine = jnp.cos(angle), jnp.sin(angle)
    cosine = jnp.concatenate([cosine, cosine], axis=1)
    sine = jnp.concatenate([-sine, sine], axis=1)
    return pl.pallas_call(
        finish_kernel,
        out_shape=jax.ShapeDtypeStruct((packed_rows(rows), LANES), jnp.bfloat16),
        in_specs=[pl.BlockSpec(memory_space=pltpu.VMEM)] * (2 + len(parts)),
        out_specs=pl.BlockSpec(memory_space=pltpu.VMEM),
        compiler_params=pltpu.CompilerParams(vmem_limit_bytes=4 * 2**20),
        name="finish",
    )(cosine, sine, *parts)


def plan_kernel(list_ref, plan_ref):
    groups, slots = list_ref.shape

    def one_group(g, at):
        def one_pair(t, at):
            first, second = list_ref[g, 2 * t], list_ref[g, 2 * t + 1]

            @pl.when(first >= 0)
            def _():
                plan_ref[1 + 3 * at] = g
                plan_ref[2 + 3 * at] = first
                plan_ref[3 + 3 * at] = second

            return at + (first >= 0).astype(jnp.int32)

        return lax.fori_loop(0, slots // 2, one_pair, at)

    plan_ref[0] = lax.fori_loop(0, groups, one_group, jnp.int32(0))


def plan_items(block_list):
    groups, slots = block_list.shape
    return pl.pallas_call(
        plan_kernel,
        out_shape=jax.ShapeDtypeStruct((1 + 3 * groups * (slots // 2),), jnp.int32),
        in_specs=[pl.BlockSpec(memory_space=pltpu.SMEM)],
        out_specs=pl.BlockSpec(memory_space=pltpu.SMEM),
        compiler_params=pltpu.CompilerParams(vmem_limit_bytes=2**20),
        name="plan",
    )(block_list)


def spread_kernel(q_ref, o_ref, wide, sem):
    groups = wide.shape[0]
    copies = [pltpu.make_async_copy(q_ref.at[pl.ds(g * BLK, BLK), :], wide.at[g], sem.at[g]) for g in range(groups)]
    for copy in copies:
        copy.start()
    width = wide.shape[2]
    for g in range(groups):
        copies[g].wait()
        for h in range(width // WIDTH):
            c = h * WIDTH
            if c % LANES:
                part = wide[g, :, c - RD : c + WIDTH]
                part = jnp.concatenate([part[:, RD:], part[:, :RD]], axis=1)
            elif c + PADDED <= width:
                part = wide[g, :, c : c + PADDED]
            else:
                part = jnp.concatenate([wide[g, :, c : c + WIDTH], jnp.zeros((BLK, RD), jnp.bfloat16)], axis=1)
            o_ref[g, h * BLK : (h + 1) * BLK, :] = part


def spread(queries):
    groups, heads = queries.shape[0] // BLK, queries.shape[1] // WIDTH
    return pl.pallas_call(
        spread_kernel,
        in_specs=[pl.BlockSpec(memory_space=pltpu.HBM)],
        out_specs=pl.BlockSpec(memory_space=pltpu.VMEM),
        out_shape=jax.ShapeDtypeStruct((groups, heads * BLK, PADDED), jnp.bfloat16),
        scratch_shapes=[
            pltpu.VMEM((groups, BLK, queries.shape[1]), jnp.bfloat16),
            pltpu.SemaphoreType.DMA((groups,)),
        ],
        compiler_params=pltpu.CompilerParams(vmem_limit_bytes=8 * 2**20),
        cost_estimate=pl.CostEstimate(flops=0, bytes_accessed=10_000_000, transcendentals=0),
        name="spread",
    )(queries)


def attend_kernel(layout, parts, chunk, plan_ref, q2, *refs):
    pieces, refs = refs[: len(layout)], refs[len(layout) :]
    out_hbm, kx, gap, s_ref, p_ref, m_ref, l_ref, acc, obuf, sem_o = refs
    groups, rows, _ = q2.shape
    heads = rows // BLK
    tile = min(TILE, rows)
    packed = packed_rows(chunk)
    pb, ka = lax.axis_index("pb"), lax.axis_index("ka")
    items = plan_ref[0]

    def out_copy(g):
        rows_out = pl.ds(pl.multiple_of(g * BLK, BLK), BLK)
        return pltpu.make_async_copy(obuf.at[g], out_hbm.at[rows_out, :], sem_o.at[g])

    gap[...] = lax.broadcasted_iota(jnp.int32, (BLK, BLK), 0) - lax.broadcasted_iota(jnp.int32, (BLK, BLK), 1)
    acc[...] = jnp.zeros_like(acc)
    kx[:, KVL:] = jnp.zeros((kx.shape[0], LANES), jnp.bfloat16)
    for piece, offsets in zip(pieces, layout):
        for at, (dk, dq) in enumerate(offsets):
            at *= packed
            row = pl.multiple_of(((ka ^ dk) * parts + (pb ^ dq)) * chunk, chunk)
            for c in range(KVL // LANES):
                kx[pl.ds(row, chunk), c * LANES : (c + 1) * LANES] = piece[at + c * chunk : at + (c + 1) * chunk, :]
            rotary = piece[at + 4 * chunk : at + packed, :]
            if chunk % 32 == 0:
                kx[pl.ds(row, chunk // 2), KVL : KVL + RD] = rotary[:, :RD]
                kx[pl.ds(row + chunk // 2, chunk // 2), KVL : KVL + RD] = rotary[:, RD:]
            else:
                kx[pl.ds(row, chunk), KVL:] = rotary

    def item(t):
        return plan_ref[1 + 3 * t], plan_ref[2 + 3 * t], plan_ref[3 + 3 * t]

    def group_of(t):
        return plan_ref[1 + 3 * t]

    def key_rows(b0, b1, width):
        cut = [pl.ds(pl.multiple_of(jnp.maximum(b, 0) * BLK, BLK), BLK) for b in (b0, b1)]
        return jnp.concatenate([kx[c, :width] for c in cut], axis=0)

    def begin():
        m_ref[...] = jnp.full_like(m_ref, LOWEST)
        l_ref[...] = jnp.zeros_like(l_ref)

    def mask(t):
        g, b0, b1 = item(t)
        bias = []
        for b in (b0, b1):
            first_seen = (jnp.where(b >= 0, b, 1 << 14) - (pb * groups + g)) * BLK
            bias.append(jnp.where(gap[...] >= first_seen, 0.0, MASKED))
        return bias

    def score(g, r, keys, bias):
        s = lax.dot_general(
            q2[g, r : r + tile, :], keys, (((1,), (1,)), ((), ())), preferred_element_type=jnp.float32
        )
        for h in range(0, tile, BLK):
            sl = slice(r + h, r + h + BLK)
            s0 = s[h : h + BLK, :BLK] + bias[0]
            s1 = s[h : h + BLK, BLK:] + bias[1]
            s_ref[sl, :BLK] = s0
            s_ref[sl, BLK:] = s1
            p_ref[sl, :] = jnp.maximum(s0, s1)

    def weigh(r):
        weights, fades = [], []
        for h in range(0, tile, BLK):
            sl = slice(r + h, r + h + BLK)
            old = m_ref[sl, :]
            new = jnp.maximum(old, jnp.max(p_ref[sl, :], axis=1, keepdims=True) * SCALE)
            fade = jnp.exp2(old - new)
            e0 = jnp.exp2(s_ref[sl, :BLK] * SCALE - new)
            e1 = jnp.exp2(s_ref[sl, BLK:] * SCALE - new)
            m_ref[sl, :] = new
            l_ref[sl, :] = l_ref[sl, :] * fade + (e0 + e1)
            weights.append(jnp.concatenate([e0.astype(jnp.bfloat16), e1.astype(jnp.bfloat16)], axis=1))
            fades.append(fade)
        return jnp.concatenate(weights, axis=0), fades

    def blend(r, weights, fades, values):
        o = jnp.dot(weights, values, preferred_element_type=jnp.float32)
        for h in range(0, tile, BLK):
            sl = slice(r + h, r + h + BLK)
            for c in range(0, KVL, LANES):
                acc[sl, c : c + LANES] = acc[sl, c : c + LANES] * fades[h // BLK] + o[h : h + BLK, c : c + LANES]

    def turn(t):
        g = group_of(t)

        @pl.when((t == items - 1) | (group_of(jnp.minimum(t + 1, items - 1)) != g))
        def _():
            for h in range(heads):
                sl = slice(h * BLK, (h + 1) * BLK)
                inverse = 1.0 / jnp.sum(l_ref[sl, :], axis=1, keepdims=True)
                obuf[g, :, h * KVL : (h + 1) * KVL] = (acc[sl, :] * inverse).astype(jnp.bfloat16)
            out_copy(g).start()
            begin()

    begin()
    g, b0, b1 = item(0)
    keys, bias = key_rows(b0, b1, PADDED), mask(0)
    for r in range(0, rows, tile):
        score(g, r, keys, bias)

    @pl.loop(0, items)
    def _(t):
        following = jnp.minimum(t + 1, items - 1)

        _, b0, b1 = item(t)
        values = key_rows(b0, b1, KVL)
        g, b0, b1 = item(following)
        keys, bias = key_rows(b0, b1, PADDED), mask(following)
        for r in range(0, rows, tile):
            weights, fades = weigh(r)
            score(g, r, keys, bias)
            blend(r, weights, fades, values)
        turn(t)

    for g in range(groups):
        out_copy(g).wait()


def attend(plan, q2, pieces, layout, parts, chunk, key_count):
    groups, rows, _ = q2.shape
    heads = rows // BLK
    f32, bf16 = jnp.float32, jnp.bfloat16
    return pl.pallas_call(
        functools.partial(attend_kernel, layout, parts, chunk),
        out_shape=jax.ShapeDtypeStruct((groups * BLK, heads * KVL), bf16),
        in_specs=[pl.BlockSpec(memory_space=pltpu.SMEM)]
        + [pl.BlockSpec(memory_space=pltpu.VMEM)] * (1 + len(pieces)),
        out_specs=pl.BlockSpec(memory_space=pltpu.HBM),
        scratch_shapes=[
            pltpu.VMEM((key_count, PADDED), bf16),
            pltpu.VMEM((BLK, BLK), jnp.int32),
            pltpu.VMEM((rows, 2 * BLK), f32),
            pltpu.VMEM((rows, LANES), f32),
            pltpu.VMEM((rows, LANES), f32),
            pltpu.VMEM((rows, LANES), f32),
            pltpu.VMEM((rows, KVL), f32),
            pltpu.VMEM((groups, BLK, heads * KVL), bf16),
            pltpu.SemaphoreType.DMA((groups,)),
        ],
        compiler_params=pltpu.CompilerParams(vmem_limit_bytes=26 * 2**20),
        cost_estimate=pl.CostEstimate(flops=16_000_000_000, bytes_accessed=12_000_000, transcendentals=6_000_000),
        name="attend",
    )(plan, q2, *pieces)


def per_device(n_pb, n_ka, tokens, kv_weight, queries, block_list):
    local_rows = tokens.shape[0]
    chunk = local_rows // n_pb
    partials = project(tokens, kv_weight, n_pb)
    arrived = [partials[0]] + [swap(partials[k], "pb", k, n_pb) for k in range(1, n_pb)]
    first_row = lax.axis_index("ka") * local_rows + lax.axis_index("pb") * chunk
    queries, plan, *arrived = lax.optimization_barrier((spread(queries), plan_items(block_list), *arrived))
    own = finish(arrived, first_row)

    far = range(2, n_ka, 2)
    ring = [0] + list(far)
    column = jnp.concatenate([own] + [swap(own, "ka", k, n_ka) for k in far], axis=0)
    if n_pb == 4:
        corner = swap(own, "pb", 3, n_pb)
        wide = [(column, 0)] + [(swap(column, "pb", k, n_pb), k) for k in (1, 2)]
        corners = jnp.concatenate([corner] + [swap(corner, "ka", k, n_ka) for k in far], axis=0)
        late = [(corners, 3)]
    else:
        wide = [(column, 0)] + [(swap(column, "pb", k, n_pb), k) for k in range(1, n_pb)]
        late = []
    held = lax.optimization_barrier([piece for piece, _ in wide])
    wide = [(piece, k) for piece, (_, k) in zip(held, wide)]
    sets = [(piece, [(d, k) for d in ring]) for piece, k in wide + late]
    sets += [(swap(piece, "ka", 1, n_ka), [(d ^ 1, k) for d, k in offsets]) for piece, offsets in sets]
    pieces = [piece for piece, _ in sets]
    layout = [offsets for _, offsets in sets]
    return attend(plan, queries, pieces, layout, n_pb, chunk, local_rows * n_ka)


def solution(mesh):
    in_specs = (P("ka", "pb"), P("pb", None), P("pb", "ka"), P("pb", None))
    out_specs = P("pb", "ka")
    return jax.shard_map(
        functools.partial(per_device, mesh.shape["pb"], mesh.shape["ka"]),
        mesh=mesh,
        in_specs=in_specs,
        out_specs=out_specs,
        check_vma=False,
    )
```

```python
import functools
import math

import jax
import jax.numpy as jnp
from jax import lax
from jax.experimental import pallas as pl
from jax.experimental.pallas import tpu as pltpu
from jax.sharding import PartitionSpec as P

KVL = 512
RD = 64
QK = 192
BLK = 128
LANES = 128
WIDTH = KVL + RD
PADDED = KVL + 2 * RD
MASKED = -1e30
LOWEST = -3e38
UNIT = BLK // 2
SENT = jnp.float32
TILE = 1024
LIMIT = 20
SCALE = math.log2(math.e) / math.sqrt(QK)


def packed_rows(rows):
    return rows * 4 + (rows // 2 if rows % 32 == 0 else rows)


def swap(x, axis_name, offset, count):
    return lax.ppermute(x, axis_name, [(i, i ^ offset) for i in range(count)])


def project_kernel(cuts, tokens_ref, weight_ref, *rest):
    outs, (tok, wgt, total, sem) = rest[:-4], rest[-4:]
    copies = []
    for t, (start, depth) in enumerate(cuts):
        cut = pl.ds(start, depth)
        pair = [
            pltpu.make_async_copy(tokens_ref.at[:, cut], tok.at[:, cut], sem.at[0, t]),
            pltpu.make_async_copy(weight_ref.at[:, cut], wgt.at[:, cut], sem.at[1, t]),
        ]
        for copy in pair:
            copy.start()
        copies.append(pair)
    for t, (start, depth) in enumerate(cuts):
        for copy in copies[t]:
            copy.wait()
        cut = slice(start, start + depth)
        part = lax.dot_general(
            tok[:, cut], wgt[:, cut], (((1,), (1,)), ((), ())), preferred_element_type=jnp.float32
        )
        total[...] = part if t == 0 else total[...] + part
    rows = outs[0].shape[0]
    me = lax.axis_index("pb")
    for k, out in enumerate(outs):
        out[...] = total[pl.ds(pl.multiple_of((me ^ k) * rows, rows), rows), :].astype(out.dtype)


def project(tokens, kv_weight, parts):
    rows, features = tokens.shape
    depth = 896
    cuts = [(start, min(depth, features - start)) for start in range(0, features, depth)]
    return pl.pallas_call(
        functools.partial(project_kernel, cuts),
        out_shape=[jax.ShapeDtypeStruct((rows // parts, WIDTH), jnp.float32 if k == 0 else SENT) for k in range(parts)],
        in_specs=[pl.BlockSpec(memory_space=pltpu.HBM)] * 2,
        out_specs=[pl.BlockSpec(memory_space=pltpu.VMEM)] * parts,
        scratch_shapes=[
            pltpu.VMEM((rows, features), jnp.bfloat16),
            pltpu.VMEM((WIDTH, features), jnp.bfloat16),
            pltpu.VMEM((rows, WIDTH), jnp.float32),
            pltpu.SemaphoreType.DMA((2, len(cuts))),
        ],
        compiler_params=pltpu.CompilerParams(vmem_limit_bytes=60 * 2**20),
        name="project",
    )(tokens, kv_weight.T)


def finish_kernel(cos_ref, sin_ref, *rest):
    parts, out = rest[:-1], rest[-1]
    total = parts[0][...]
    for part in parts[1:]:
        total = total + part[...].astype(jnp.float32)
    rows = total.shape[0]
    latent = total[:, :KVL]
    latent = latent * lax.rsqrt(jnp.mean(latent * latent, axis=-1, keepdims=True) + 1e-06)
    for c in range(KVL // LANES):
        out[c * rows : (c + 1) * rows, :] = latent[:, c * LANES : (c + 1) * LANES].astype(jnp.bfloat16)
    rotary = total[:, KVL:]
    half = RD // 2
    turned = jnp.concatenate([rotary[:, half:], rotary[:, :half]], axis=1)
    rotary = rotary * cos_ref[...] + turned * sin_ref[...]
    if rows % 32 == 0:
        both = jnp.concatenate([rotary[: rows // 2], rotary[rows // 2 :]], axis=1)
    else:
        both = jnp.concatenate([rotary, jnp.zeros_like(rotary)], axis=1)
    out[4 * rows :, :] = both.astype(jnp.bfloat16)


def finish(parts, first_row):
    rows = parts[0].shape[0]
    half = RD // 2
    freq = jnp.exp(jnp.arange(half, dtype=jnp.float32) * (-2.0 * math.log(10000.0) / RD))
    position = (first_row + jnp.arange(rows, dtype=jnp.int32)).astype(jnp.float32)
    angle = position[:, None] * freq[None, :]
    cosine, sine = jnp.cos(angle), jnp.sin(angle)
    cosine = jnp.concatenate([cosine, cosine], axis=1)
    sine = jnp.concatenate([-sine, sine], axis=1)
    return pl.pallas_call(
        finish_kernel,
        out_shape=jax.ShapeDtypeStruct((packed_rows(rows), LANES), jnp.bfloat16),
        in_specs=[pl.BlockSpec(memory_space=pltpu.VMEM)] * (2 + len(parts)),
        out_specs=pl.BlockSpec(memory_space=pltpu.VMEM),
        compiler_params=pltpu.CompilerParams(vmem_limit_bytes=4 * 2**20),
        name="finish",
    )(cosine, sine, *parts)


def plan_kernel(phases, units, list_ref, plan_ref):
    groups, slots = list_ref.shape
    side = lax.axis_index("pb") // 2
    width = slots + 4
    base = entry_base(phases, groups, slots, units)
    counts = [[], [], []]
    for g in range(groups):
        at = [jnp.int32(0), jnp.int32(0), jnp.int32(0)]
        for t in range(slots):
            b = list_ref[g, t]
            live = (b >= 0).astype(jnp.int32)
            kind = (b & 1) ^ side
            plan_ref[base + g * width + t] = b
            for k in range(2):
                if phases > 1:
                    plan_ref[base + ((1 + k) * groups + g) * width + at[1 + k]] = b
                    at[1 + k] = at[1 + k] + jnp.where(kind == k, live, 0)
            at[0] = at[0] + live
        for k in range(3 if phases > 1 else 1):
            counts[k].append(at[k])
            for t in range(4):
                plan_ref[base + (k * groups + g) * width + at[k] + t] = -1
    for p in range(phases):
        kind = phase_kind(phases, p)
        step = 4 // units[p]
        where = item_base(phases, groups, slots, units, p)
        total = jnp.int32(0)
        for g in range(groups):
            n = (counts[kind][g] + step - 1) // step
            if p == phases - 1 or g == 0:
                n = jnp.maximum(n, 1)

            @pl.loop(0, n)
            def _(k, g=g, total=total):
                plan_ref[where + 1 + 2 * (total + k)] = g
                plan_ref[where + 2 + 2 * (total + k)] = base + (kind * groups + g) * width + k * step

            total = total + n
        plan_ref[where] = total


def phase_kind(phases, phase):
    return 0 if phases == 1 else (1, 0, 2)[phase]


def item_base(phases, groups, slots, units, phase):
    return sum(1 + 2 * (groups * (slots * u // 4 + 1) + 1) for u in units[:phase])


def entry_base(phases, groups, slots, units):
    return item_base(phases, groups, slots, units, phases)


def plan_items(block_list, phases, units):
    groups, slots = block_list.shape
    size = entry_base(phases, groups, slots, units) + (3 if phases > 1 else 1) * groups * (slots + 4)
    return pl.pallas_call(
        functools.partial(plan_kernel, phases, units),
        out_shape=jax.ShapeDtypeStruct((size,), jnp.int32),
        in_specs=[pl.BlockSpec(memory_space=pltpu.SMEM)],
        out_specs=pl.BlockSpec(memory_space=pltpu.SMEM),
        compiler_params=pltpu.CompilerParams(vmem_limit_bytes=2**20),
        name="plan",
    )(block_list)


def spread_kernel(q_ref, o_ref, wide, sem):
    groups = wide.shape[0]
    copies = [pltpu.make_async_copy(q_ref.at[pl.ds(g * BLK, BLK), :], wide.at[g], sem.at[g]) for g in range(groups)]
    for copy in copies:
        copy.start()
    width = wide.shape[2]
    for g in range(groups):
        copies[g].wait()
        for h in range(width // WIDTH):
            c = h * WIDTH
            if c % LANES:
                part = wide[g, :, c - RD : c + WIDTH]
                part = jnp.concatenate([part[:, RD:], part[:, :RD]], axis=1)
            elif c + PADDED <= width:
                part = wide[g, :, c : c + PADDED]
            else:
                part = jnp.concatenate([wide[g, :, c : c + WIDTH], jnp.zeros((BLK, RD), jnp.bfloat16)], axis=1)
            for c in range(PADDED // LANES):
                o_ref[g, c, h * BLK : (h + 1) * BLK, :] = part[:, c * LANES : (c + 1) * LANES]


def spread(queries):
    groups, heads = queries.shape[0] // BLK, queries.shape[1] // WIDTH
    return pl.pallas_call(
        spread_kernel,
        in_specs=[pl.BlockSpec(memory_space=pltpu.HBM)],
        out_specs=pl.BlockSpec(memory_space=pltpu.VMEM),
        out_shape=jax.ShapeDtypeStruct((groups, PADDED // LANES, heads * BLK, LANES), jnp.bfloat16),
        scratch_shapes=[
            pltpu.VMEM((groups, BLK, queries.shape[1]), jnp.bfloat16),
            pltpu.SemaphoreType.DMA((groups,)),
        ],
        compiler_params=pltpu.CompilerParams(vmem_limit_bytes=8 * 2**20),
        cost_estimate=pl.CostEstimate(flops=0, bytes_accessed=10_000_000, transcendentals=0),
        name="spread",
    )(queries)


def attend_kernel(layout, members, parts, chunk, where, units, first, last, plan_ref, q2, *refs):
    pieces, refs = refs[: len(layout)], list(refs[len(layout) :])
    if not first:
        refs = refs[3:]
    if last:
        out_hbm = refs.pop(0)
    m_ref, l_ref, acc = refs[:3]
    kx, gap, s_ref, p_ref = refs[3:7]
    if last:
        obuf, sem_o = refs[7:]
    groups, _, rows, _ = q2.shape
    heads = rows // BLK
    tile = min(TILE, rows)
    packed = packed_rows(chunk)
    pb, ka = lax.axis_index("pb"), lax.axis_index("ka")
    items = plan_ref[where]
    per_group = parts * chunk // UNIT

    row = lax.broadcasted_iota(jnp.int32, (BLK, BLK), 0)
    column = lax.broadcasted_iota(jnp.int32, (BLK, BLK), 1)
    gap[...] = row - column % UNIT
    if first:
        m_ref[...] = jnp.full_like(m_ref, LOWEST)
        l_ref[...] = jnp.zeros_like(l_ref)
        acc[...] = jnp.zeros_like(acc)
    kx[KVL // LANES] = jnp.zeros(kx.shape[1:], jnp.bfloat16)
    for piece, offsets in zip(pieces, layout):
        for at, (dk, dq) in enumerate(offsets):
            at *= packed
            if members is None:
                row = ((ka ^ dk) * parts + (pb ^ dq)) * chunk
            else:
                row = ((ka ^ dk) * len(members) + members.index(dq)) * chunk
            row = pl.multiple_of(row, chunk)
            for c in range(KVL // LANES):
                kx[c, pl.ds(row, chunk), :] = piece[at + c * chunk : at + (c + 1) * chunk, :]
            rotary = piece[at + 4 * chunk : at + packed, :]
            if chunk % 32 == 0:
                kx[KVL // LANES, pl.ds(row, chunk // 2), :RD] = rotary[:, :RD]
                kx[KVL // LANES, pl.ds(row + chunk // 2, chunk // 2), :RD] = rotary[:, RD:]
            else:
                kx[KVL // LANES, pl.ds(row, chunk), :] = rotary

    def group_of(t):
        return plan_ref[where + 1 + 2 * t]

    def key_units(t):
        entry = plan_ref[where + 2 + 2 * t]
        found = []
        for i in range(4):
            b = plan_ref[entry + i // units]
            known = jnp.maximum(b, 0)
            if members is None:
                unit = known * 2 + i % units
                row = unit
            else:
                index = jnp.int32(0)
                seat = pb ^ members[0]
                if len(members) == 2:
                    index = (known & 1) ^ (pb // 2)
                    seat = jnp.where(index == 0, seat, pb ^ members[1])
                unit = known * 2 + seat % 2
                row = known // (per_group // 2) * len(members) + index
            found.append((pl.multiple_of(row * UNIT, UNIT), jnp.where(b >= 0, unit * UNIT, 1 << 24)))
        return found

    def key_rows(found, width):
        columns = range(width // LANES)
        units = [jnp.concatenate([kx[c, pl.ds(row, UNIT), :] for c in columns], axis=1) for row, _ in found]
        return jnp.concatenate(units, axis=0)

    def mask(found, g):
        here = (pb * groups + g) * BLK
        left = lax.broadcasted_iota(jnp.int32, (BLK, BLK), 1) < UNIT
        bias = []
        for i in range(2):
            seen = [found[2 * i + k][1] - here for k in range(2)]
            bias.append(jnp.where(gap[...] >= jnp.where(left, seen[0], seen[1]), 0.0, MASKED))
        return bias

    def score(g, r, keys, bias):
        s = lax.dot_general(
            jnp.concatenate([q2[g, c, r : r + tile, :] for c in range(PADDED // LANES)], axis=1), keys, (((1,), (1,)), ((), ())), preferred_element_type=jnp.float32
        )
        for h in range(0, tile, BLK):
            sl = slice(r + h, r + h + BLK)
            s0 = s[h : h + BLK, :BLK] + bias[0]
            s1 = s[h : h + BLK, BLK:] + bias[1]
            s_ref[sl, :BLK] = s0
            s_ref[sl, BLK:] = s1
            p_ref[sl, :] = jnp.maximum(s0, s1)

    def weigh(g, r):
        weights, fades = [], []
        for h in range(0, tile, BLK):
            sl = slice(r + h, r + h + BLK)
            old = m_ref[g, sl, :]
            new = jnp.maximum(old, jnp.max(p_ref[sl, :], axis=1, keepdims=True) * SCALE)
            fade = jnp.exp2(old - new)
            e0 = jnp.exp2(s_ref[sl, :BLK] * SCALE - new)
            e1 = jnp.exp2(s_ref[sl, BLK:] * SCALE - new)
            m_ref[g, sl, :] = new
            l_ref[g, sl, :] = l_ref[g, sl, :] * fade + (e0 + e1)
            weights.append(jnp.concatenate([e0.astype(jnp.bfloat16), e1.astype(jnp.bfloat16)], axis=1))
            fades.append(fade)
        return jnp.concatenate(weights, axis=0), fades

    def blend(g, r, weights, fades, values):
        o = jnp.dot(weights, values, preferred_element_type=jnp.float32)
        for h in range(0, tile, BLK):
            sl = slice(r + h, r + h + BLK)
            for c in range(0, KVL, LANES):
                acc[g, sl, c : c + LANES] = (
                    acc[g, sl, c : c + LANES] * fades[h // BLK] + o[h : h + BLK, c : c + LANES]
                )

    def out_copy(g):
        rows_out = pl.ds(pl.multiple_of(g * BLK, BLK), BLK)
        return pltpu.make_async_copy(obuf.at[g], out_hbm.at[rows_out, :], sem_o.at[g])

    def turn(t, g):
        @pl.when((t == items - 1) | (group_of(jnp.minimum(t + 1, items - 1)) != g))
        def _():
            for h in range(heads):
                sl = slice(h * BLK, (h + 1) * BLK)
                inverse = 1.0 / jnp.sum(l_ref[g, sl, :], axis=1, keepdims=True)
                obuf[g, :, h * KVL : (h + 1) * KVL] = (acc[g, sl, :] * inverse).astype(jnp.bfloat16)
            out_copy(g).start()

    def ahead(t):
        found, g = key_units(t), group_of(t)
        keys, bias = key_rows(found, PADDED), mask(found, g)
        for r in range(0, rows, tile):
            score(g, r, keys, bias)

    def step(t, more):
        g = group_of(t)
        values = key_rows(key_units(t), KVL)
        parts_now = [weigh(g, r) for r in range(0, rows, tile)]
        if more:
            ahead(t + 1)
        for r, (weights, fades) in zip(range(0, rows, tile), parts_now):
            blend(g, r, weights, fades, values)

    ahead(0)

    if last:

        @pl.loop(0, items - 1)
        def _(t):
            step(t, True)
            turn(t, group_of(t))
    else:

        @pl.loop(0, (items - 1) // 2)
        def _(i):
            step(2 * i, True)
            step(2 * i + 1, True)

        @pl.when((items > 1) & (items % 2 == 0))
        def _():
            step(items - 2, True)

    step(items - 1, False)
    if last:
        turn(items - 1, group_of(items - 1))

    if last:
        for g in range(groups):
            out_copy(g).wait()


def attend(plan, where, units, q2, sets, members, parts, chunk, key_count, state, last):
    pieces, layout = [piece for piece, _ in sets], [offsets for _, offsets in sets]
    groups, _, rows, _ = q2.shape
    heads = rows // BLK
    f32, bf16 = jnp.float32, jnp.bfloat16
    vmem = pl.BlockSpec(memory_space=pltpu.VMEM)
    shapes = [(groups, rows, LANES), (groups, rows, LANES), (groups, rows, KVL)]
    first = not state
    out_shape = [jax.ShapeDtypeStruct(s, f32) for s in shapes]
    out_specs = [vmem] * 3
    if last:
        out_shape = [jax.ShapeDtypeStruct((groups * BLK, heads * KVL), bf16)] + out_shape
        out_specs = [pl.BlockSpec(memory_space=pltpu.HBM)] + out_specs
    scratch = [
        pltpu.VMEM((PADDED // LANES, key_count, LANES), bf16),
        pltpu.VMEM((BLK, BLK), jnp.int32),
        pltpu.VMEM((rows, 2 * BLK), f32),
        pltpu.VMEM((rows, LANES), f32),
    ]
    if last:
        scratch += [pltpu.VMEM((groups, BLK, heads * KVL), bf16), pltpu.SemaphoreType.DMA((groups,))]
    at = 2 + len(pieces)
    result = pl.pallas_call(
        functools.partial(attend_kernel, layout, members, parts, chunk, where, units, first, last),
        out_shape=out_shape,
        in_specs=[pl.BlockSpec(memory_space=pltpu.SMEM)] + [vmem] * (1 + len(pieces) + len(state)),
        out_specs=out_specs,
        input_output_aliases={at + i: int(last) + i for i in range(len(state))},
        scratch_shapes=scratch,
        compiler_params=pltpu.CompilerParams(vmem_limit_bytes=LIMIT * 2**20),
        cost_estimate=pl.CostEstimate(flops=5_000_000_000, bytes_accessed=4_000_000, transcendentals=2_000_000),
        name="attend",
    )(plan, q2, *pieces, *state)
    return result[0] if last else result


def per_device(n_pb, n_ka, tokens, kv_weight, queries, block_list):
    local_rows = tokens.shape[0]
    chunk = local_rows // n_pb
    key_count = local_rows * n_ka
    far = range(2, n_ka, 2)
    ring = [0] + list(far)
    phased = n_pb == 4 and chunk == UNIT

    def swap_core(piece, k):
        return swap(piece, "ka", 1, n_ka), [(d ^ 1, k) for d in ring]

    def swap_both(piece, over, core):
        away = over * n_ka + core
        return lax.ppermute(piece, ("pb", "ka"), [(i, i ^ away) for i in range(n_pb * n_ka)])

    partials = project(tokens, kv_weight, n_pb)
    arrived = [partials[0]] + [swap(partials[k], "pb", k, n_pb) for k in range(1, n_pb)]
    first_row = lax.axis_index("ka") * local_rows + lax.axis_index("pb") * chunk
    phases, units = (3, (1, 1, 1)) if phased else (1, (2,))
    where = [item_base(phases, *block_list.shape, units, p) for p in range(phases)]
    plan = plan_items(block_list, phases, units)
    queries, plan, *arrived = lax.optimization_barrier((spread(queries), plan, *arrived))
    own = finish(arrived, first_row)
    column = jnp.concatenate([own] + [swap(own, "ka", k, n_ka) for k in far], axis=0)

    if not phased:
        sets = [(column, [(d, 0) for d in ring])]
        sets += [(swap(column, "pb", k, n_pb), [(d, k) for d in ring]) for k in range(1, n_pb)]
        sets += [swap_core(piece, offsets[0][1]) for piece, offsets in sets]
        return attend(plan, where[0], 2, queries, sets, None, n_pb, chunk, key_count, [], True)

    beside = [swap(column, "pb", k, n_pb) for k in (1, 2)]
    other, _ = swap_core(column, 0)
    sets = [(column, [(d, 0) for d in ring]), (other, [(d ^ 1, 0) for d in ring])]
    state = attend(plan, where[0], 1, queries, sets, [0], n_pb, chunk, key_count // 4, [], False)

    *state, x, y = lax.optimization_barrier((*state, *beside))
    sets = [(x, [(d, 1) for d in ring]), (y, [(d, 2) for d in ring])]
    sets += [swap_core(x, 1), swap_core(y, 2)]
    half = len(ring) // 2
    cut = half * packed_rows(chunk)
    corner = []
    for core in (0, 1):
        corner.append((swap_both(y[:cut], 1, core), [(d ^ core, 3) for d in ring[:half]]))
        corner.append((swap_both(x[cut:], 2, core), [(d ^ core, 3) for d in ring[half:]]))
    state = attend(plan, where[1], 1, queries, sets, [1, 2], n_pb, chunk, key_count // 2, list(state), False)

    held = lax.optimization_barrier((*state, *[piece for piece, _ in corner]))
    state, corner = list(held[:3]), [(piece, offsets) for piece, (_, offsets) in zip(held[3:], corner)]
    return attend(plan, where[2], 1, queries, corner, [3], n_pb, chunk, key_count // 4, state, True)


def solution(mesh):
    in_specs = (P("ka", "pb"), P("pb", None), P("pb", "ka"), P("pb", None))
    out_specs = P("pb", "ka")
    return jax.shard_map(
        functools.partial(per_device, mesh.shape["pb"], mesh.shape["ka"]),
        mesh=mesh,
        in_specs=in_specs,
        out_specs=out_specs,
        check_vma=False,
    )
```

```python
import functools
import math

import jax
import jax.numpy as jnp
from jax import lax
from jax.experimental import pallas as pl
from jax.experimental.pallas import tpu as pltpu
from jax.sharding import PartitionSpec as P

KVL = 512
RD = 64
QK = 192
BLK = 128
LANES = 128
WIDTH = KVL + RD
PADDED = KVL + 2 * RD
MASKED = -1e30
LOWEST = -3e38
UNIT = BLK // 2
SENT = jnp.float32
TILE = 1024
SPREAD_LIMIT = 2
LIMIT = 20
SCALE = math.log2(math.e) / math.sqrt(QK)


def packed_rows(rows):
    return rows * 4 + (rows // 2 if rows % 32 == 0 else rows)


def swap(x, axis_name, offset, count):
    return lax.ppermute(x, axis_name, [(i, i ^ offset) for i in range(count)])


def project_kernel(cuts, tokens_ref, weight_ref, *rest):
    outs, (tok, wgt, total, sem) = rest[:-4], rest[-4:]
    copies = []
    for t, (start, depth) in enumerate(cuts):
        cut = pl.ds(start, depth)
        pair = [
            pltpu.make_async_copy(tokens_ref.at[:, cut], tok.at[:, cut], sem.at[0, t]),
            pltpu.make_async_copy(weight_ref.at[:, cut], wgt.at[:, cut], sem.at[1, t]),
        ]
        for copy in pair:
            copy.start()
        copies.append(pair)
    for t, (start, depth) in enumerate(cuts):
        for copy in copies[t]:
            copy.wait()
        cut = slice(start, start + depth)
        part = lax.dot_general(
            tok[:, cut], wgt[:, cut], (((1,), (1,)), ((), ())), preferred_element_type=jnp.float32
        )
        total[...] = part if t == 0 else total[...] + part
    rows = outs[0].shape[0]
    me = lax.axis_index("pb")
    for k, out in enumerate(outs):
        out[...] = total[pl.ds(pl.multiple_of((me ^ k) * rows, rows), rows), :].astype(out.dtype)


def project(tokens, kv_weight, parts):
    rows, features = tokens.shape
    depth = 896
    cuts = [(start, min(depth, features - start)) for start in range(0, features, depth)]
    return pl.pallas_call(
        functools.partial(project_kernel, cuts),
        out_shape=[jax.ShapeDtypeStruct((rows // parts, WIDTH), jnp.float32 if k == 0 else SENT) for k in range(parts)],
        in_specs=[pl.BlockSpec(memory_space=pltpu.HBM)] * 2,
        out_specs=[pl.BlockSpec(memory_space=pltpu.VMEM)] * parts,
        scratch_shapes=[
            pltpu.VMEM((rows, features), jnp.bfloat16),
            pltpu.VMEM((WIDTH, features), jnp.bfloat16),
            pltpu.VMEM((rows, WIDTH), jnp.float32),
            pltpu.SemaphoreType.DMA((2, len(cuts))),
        ],
        compiler_params=pltpu.CompilerParams(vmem_limit_bytes=60 * 2**20),
        name="project",
    )(tokens, kv_weight.T)


def finish_kernel(cos_ref, sin_ref, *rest):
    parts, out = rest[:-1], rest[-1]
    total = parts[0][...]
    for part in parts[1:]:
        total = total + part[...].astype(jnp.float32)
    rows = total.shape[0]
    latent = total[:, :KVL]
    latent = latent * lax.rsqrt(jnp.mean(latent * latent, axis=-1, keepdims=True) + 1e-06)
    for c in range(KVL // LANES):
        out[c * rows : (c + 1) * rows, :] = latent[:, c * LANES : (c + 1) * LANES].astype(jnp.bfloat16)
    rotary = total[:, KVL:]
    half = RD // 2
    turned = jnp.concatenate([rotary[:, half:], rotary[:, :half]], axis=1)
    rotary = rotary * cos_ref[...] + turned * sin_ref[...]
    if rows % 32 == 0:
        both = jnp.concatenate([rotary[: rows // 2], rotary[rows // 2 :]], axis=1)
    else:
        both = jnp.concatenate([rotary, jnp.zeros_like(rotary)], axis=1)
    out[4 * rows :, :] = both.astype(jnp.bfloat16)


def finish(parts, first_row):
    rows = parts[0].shape[0]
    half = RD // 2
    freq = jnp.exp(jnp.arange(half, dtype=jnp.float32) * (-2.0 * math.log(10000.0) / RD))
    position = (first_row + jnp.arange(rows, dtype=jnp.int32)).astype(jnp.float32)
    angle = position[:, None] * freq[None, :]
    cosine, sine = jnp.cos(angle), jnp.sin(angle)
    cosine = jnp.concatenate([cosine, cosine], axis=1)
    sine = jnp.concatenate([-sine, sine], axis=1)
    return pl.pallas_call(
        finish_kernel,
        out_shape=jax.ShapeDtypeStruct((packed_rows(rows), LANES), jnp.bfloat16),
        in_specs=[pl.BlockSpec(memory_space=pltpu.VMEM)] * (2 + len(parts)),
        out_specs=pl.BlockSpec(memory_space=pltpu.VMEM),
        compiler_params=pltpu.CompilerParams(vmem_limit_bytes=4 * 2**20),
        name="finish",
    )(cosine, sine, *parts)


def plan_kernel(phases, units, list_ref, plan_ref):
    groups, slots = list_ref.shape
    side = lax.axis_index("pb") // 2
    width = slots + 4
    base = entry_base(phases, groups, slots, units)
    counts = [[], [], []]
    for g in range(groups):
        at = [jnp.int32(0), jnp.int32(0), jnp.int32(0)]
        for t in range(slots):
            b = list_ref[g, t]
            live = (b >= 0).astype(jnp.int32)
            kind = (b & 1) ^ side
            plan_ref[base + g * width + t] = b
            for k in range(2):
                if phases > 1:
                    plan_ref[base + ((1 + k) * groups + g) * width + at[1 + k]] = b
                    at[1 + k] = at[1 + k] + jnp.where(kind == k, live, 0)
            at[0] = at[0] + live
        for k in range(3 if phases > 1 else 1):
            counts[k].append(at[k])
            for t in range(4):
                plan_ref[base + (k * groups + g) * width + at[k] + t] = -1
    for p in range(phases):
        kind = phase_kind(phases, p)
        step = 4 // units[p]
        where = item_base(phases, groups, slots, units, p)
        total = jnp.int32(0)
        for g in range(groups):
            n = (counts[kind][g] + step - 1) // step
            if p == phases - 1 or g == 0:
                n = jnp.maximum(n, 1)

            @pl.loop(0, n)
            def _(k, g=g, total=total):
                plan_ref[where + 1 + 2 * (total + k)] = g
                plan_ref[where + 2 + 2 * (total + k)] = base + (kind * groups + g) * width + k * step

            total = total + n
        plan_ref[where] = total


def phase_kind(phases, phase):
    return 0 if phases == 1 else (1, 0, 2)[phase]


def item_base(phases, groups, slots, units, phase):
    return sum(1 + 2 * (groups * (slots * u // 4 + 1) + 1) for u in units[:phase])


def entry_base(phases, groups, slots, units):
    return item_base(phases, groups, slots, units, phases)


def plan_items(block_list, phases, units):
    groups, slots = block_list.shape
    size = entry_base(phases, groups, slots, units) + (3 if phases > 1 else 1) * groups * (slots + 4)
    return pl.pallas_call(
        functools.partial(plan_kernel, phases, units),
        out_shape=jax.ShapeDtypeStruct((size,), jnp.int32),
        in_specs=[pl.BlockSpec(memory_space=pltpu.SMEM)],
        out_specs=pl.BlockSpec(memory_space=pltpu.SMEM),
        compiler_params=pltpu.CompilerParams(vmem_limit_bytes=2**20),
        name="plan",
    )(block_list)


def spread_kernel(q_ref, o_ref):
    width = q_ref.shape[1]
    for g in range(o_ref.shape[0]):
        rows = slice(g * BLK, (g + 1) * BLK)
        for h in range(width // WIDTH):
            c = h * WIDTH
            if c % LANES:
                part = q_ref[rows, c - RD : c + WIDTH]
                part = jnp.concatenate([part[:, RD:], part[:, :RD]], axis=1)
            elif c + PADDED <= width:
                part = q_ref[rows, c : c + PADDED]
            else:
                part = jnp.concatenate([q_ref[rows, c : c + WIDTH], jnp.zeros((BLK, RD), jnp.bfloat16)], axis=1)
            for c in range(PADDED // LANES):
                o_ref[g, c, h * BLK : (h + 1) * BLK, :] = part[:, c * LANES : (c + 1) * LANES]


def spread(queries):
    groups, heads = queries.shape[0] // BLK, queries.shape[1] // WIDTH
    vmem = pl.BlockSpec(memory_space=pltpu.VMEM)
    return pl.pallas_call(
        spread_kernel,
        in_specs=[vmem],
        out_specs=vmem,
        out_shape=jax.ShapeDtypeStruct((groups, PADDED // LANES, heads * BLK, LANES), jnp.bfloat16),
        compiler_params=pltpu.CompilerParams(vmem_limit_bytes=SPREAD_LIMIT * 2**20),
        cost_estimate=pl.CostEstimate(flops=0, bytes_accessed=10_000_000, transcendentals=0),
        name="spread",
    )(queries)


def pick_kernel(cut, x, y, other_x, other_y, near, far):
    near[:cut, :] = y[:cut, :]
    near[cut:, :] = other_y[:cut, :]
    far[: far.shape[0] // 2, :] = x[cut:, :]
    far[far.shape[0] // 2 :, :] = other_x[cut:, :]


def pick(cut, x, y, other_x, other_y):
    vmem = pl.BlockSpec(memory_space=pltpu.VMEM)
    return pl.pallas_call(
        functools.partial(pick_kernel, cut),
        out_shape=[
            jax.ShapeDtypeStruct((2 * cut, LANES), jnp.bfloat16),
            jax.ShapeDtypeStruct((2 * (x.shape[0] - cut), LANES), jnp.bfloat16),
        ],
        in_specs=[vmem] * 4,
        out_specs=[vmem] * 2,
        compiler_params=pltpu.CompilerParams(vmem_limit_bytes=2**20),
        name="pick",
    )(x, y, other_x, other_y)


def clear_kernel(ready_ref, m_ref, l_ref, acc):
    m_ref[...] = jnp.full_like(m_ref, LOWEST)
    l_ref[...] = jnp.zeros_like(l_ref)
    acc[...] = jnp.zeros_like(acc)


def clear(ready, groups, rows):
    shapes = [(groups, rows, LANES), (groups, rows, LANES), (groups, rows, KVL)]
    return pl.pallas_call(
        clear_kernel,
        out_shape=[jax.ShapeDtypeStruct(s, jnp.float32) for s in shapes],
        in_specs=[pl.BlockSpec(memory_space=pl.ANY)],
        out_specs=[pl.BlockSpec(memory_space=pltpu.VMEM)] * 3,
        compiler_params=pltpu.CompilerParams(vmem_limit_bytes=2**20),
        name="clear",
    )(ready)


def attend_kernel(layout, members, parts, chunk, where, units, unroll, last, plan_ref, q2, *refs):
    pieces, refs = refs[: len(layout)], list(refs[len(layout) :])
    refs = refs[3:]
    if last:
        out_hbm = refs.pop(0)
    m_ref, l_ref, acc = refs[:3]
    kx, gap, s_ref, p_ref = refs[3:7]
    if last:
        obuf, sem_o = refs[7:]
    groups, _, rows, _ = q2.shape
    heads = rows // BLK
    tile = min(TILE, rows)
    packed = packed_rows(chunk)
    pb, ka = lax.axis_index("pb"), lax.axis_index("ka")
    items = plan_ref[where]
    per_group = parts * chunk // UNIT

    row = lax.broadcasted_iota(jnp.int32, (BLK, BLK), 0)
    column = lax.broadcasted_iota(jnp.int32, (BLK, BLK), 1)
    gap[...] = row - column % UNIT
    kx[KVL // LANES] = jnp.zeros(kx.shape[1:], jnp.bfloat16)
    for piece, offsets in zip(pieces, layout):
        for at, (dk, dq) in enumerate(offsets):
            at *= packed
            if members is None:
                row = ((ka ^ dk) * parts + (pb ^ dq)) * chunk
            else:
                row = ((ka ^ dk) * len(members) + members.index(dq)) * chunk
            row = pl.multiple_of(row, chunk)
            for c in range(KVL // LANES):
                kx[c, pl.ds(row, chunk), :] = piece[at + c * chunk : at + (c + 1) * chunk, :]
            rotary = piece[at + 4 * chunk : at + packed, :]
            if chunk % 32 == 0:
                kx[KVL // LANES, pl.ds(row, chunk // 2), :RD] = rotary[:, :RD]
                kx[KVL // LANES, pl.ds(row + chunk // 2, chunk // 2), :RD] = rotary[:, RD:]
            else:
                kx[KVL // LANES, pl.ds(row, chunk), :] = rotary

    def group_of(t):
        return plan_ref[where + 1 + 2 * t]

    def key_units(t):
        entry = plan_ref[where + 2 + 2 * t]
        found = []
        for i in range(4):
            b = plan_ref[entry + i // units]
            known = jnp.maximum(b, 0)
            if members is None:
                unit = known * 2 + i % units
                row = unit
            else:
                index = jnp.int32(0)
                seat = pb ^ members[0]
                if len(members) == 2:
                    index = (known & 1) ^ (pb // 2)
                    seat = jnp.where(index == 0, seat, pb ^ members[1])
                unit = known * 2 + seat % 2
                row = known // (per_group // 2) * len(members) + index
            found.append((pl.multiple_of(row * UNIT, UNIT), jnp.where(b >= 0, unit * UNIT, 1 << 24)))
        return found

    def key_rows(found, width):
        columns = range(width // LANES)
        units = [jnp.concatenate([kx[c, pl.ds(row, UNIT), :] for c in columns], axis=1) for row, _ in found]
        return jnp.concatenate(units, axis=0)

    def mask(found, g):
        here = (pb * groups + g) * BLK
        left = lax.broadcasted_iota(jnp.int32, (BLK, BLK), 1) < UNIT
        bias = []
        for i in range(2):
            seen = [found[2 * i + k][1] - here for k in range(2)]
            bias.append(jnp.where(gap[...] >= jnp.where(left, seen[0], seen[1]), 0.0, MASKED))
        return bias

    def score(g, r, keys, bias):
        s = lax.dot_general(
            jnp.concatenate([q2[g, c, r : r + tile, :] for c in range(PADDED // LANES)], axis=1), keys, (((1,), (1,)), ((), ())), preferred_element_type=jnp.float32
        )
        for h in range(0, tile, BLK):
            sl = slice(r + h, r + h + BLK)
            s0 = s[h : h + BLK, :BLK] + bias[0]
            s1 = s[h : h + BLK, BLK:] + bias[1]
            s_ref[sl, :BLK] = s0
            s_ref[sl, BLK:] = s1
            p_ref[sl, :] = jnp.maximum(s0, s1)

    def weigh(g, r):
        weights, fades = [], []
        for h in range(0, tile, BLK):
            sl = slice(r + h, r + h + BLK)
            old = m_ref[g, sl, :]
            new = jnp.maximum(old, jnp.max(p_ref[sl, :], axis=1, keepdims=True) * SCALE)
            fade = jnp.exp2(old - new)
            e0 = jnp.exp2(s_ref[sl, :BLK] * SCALE - new)
            e1 = jnp.exp2(s_ref[sl, BLK:] * SCALE - new)
            m_ref[g, sl, :] = new
            l_ref[g, sl, :] = l_ref[g, sl, :] * fade + (e0 + e1)
            weights.append(jnp.concatenate([e0.astype(jnp.bfloat16), e1.astype(jnp.bfloat16)], axis=1))
            fades.append(fade)
        return jnp.concatenate(weights, axis=0), fades

    def blend(g, r, weights, fades, values):
        o = jnp.dot(weights, values, preferred_element_type=jnp.float32)
        for h in range(0, tile, BLK):
            sl = slice(r + h, r + h + BLK)
            for c in range(0, KVL, LANES):
                acc[g, sl, c : c + LANES] = (
                    acc[g, sl, c : c + LANES] * fades[h // BLK] + o[h : h + BLK, c : c + LANES]
                )

    def out_copy(g):
        rows_out = pl.ds(pl.multiple_of(g * BLK, BLK), BLK)
        return pltpu.make_async_copy(obuf.at[g], out_hbm.at[rows_out, :], sem_o.at[g])

    def end(g):
        for h in range(heads):
            sl = slice(h * BLK, (h + 1) * BLK)
            inverse = 1.0 / jnp.sum(l_ref[g, sl, :], axis=1, keepdims=True)
            obuf[g, :, h * KVL : (h + 1) * KVL] = (acc[g, sl, :] * inverse).astype(jnp.bfloat16)
        out_copy(g).start()

    def turn(t, g):
        @pl.when(group_of(t + 1) != g)
        def _():
            end(g)

    def ahead(t):
        found, g = key_units(t), group_of(t)
        keys, bias = key_rows(found, PADDED), mask(found, g)
        for r in range(0, rows, tile):
            score(g, r, keys, bias)

    def step(t, more):
        g = group_of(t)
        values = key_rows(key_units(t), KVL)
        parts_now = [weigh(g, r) for r in range(0, rows, tile)]
        if more:
            ahead(t + 1)
        for r, (weights, fades) in zip(range(0, rows, tile), parts_now):
            blend(g, r, weights, fades, values)

    turns = items - 1

    def steps(start, count):
        for k in range(count):
            step(start + k, True)
        if last:
            for k in range(count):
                turn(start + k, group_of(start + k))

    ahead(0)

    @pl.loop(0, turns // unroll)
    def _(i):
        steps(unroll * i, unroll)

    width = unroll
    while width > 1:
        width //= 2

        @pl.when((turns & width) != 0)
        def _(width=width):
            steps(turns // (2 * width) * (2 * width), width)

    step(turns, False)
    if last:
        end(group_of(turns))

    if last:
        for g in range(groups):
            out_copy(g).wait()


def attend(plan, where, units, q2, sets, members, parts, chunk, key_count, state, last, unroll=2, flops=5_000_000_000):
    pieces, layout = [piece for piece, _ in sets], [offsets for _, offsets in sets]
    groups, _, rows, _ = q2.shape
    heads = rows // BLK
    f32, bf16 = jnp.float32, jnp.bfloat16
    vmem = pl.BlockSpec(memory_space=pltpu.VMEM)
    shapes = [(groups, rows, LANES), (groups, rows, LANES), (groups, rows, KVL)]
    out_shape = [jax.ShapeDtypeStruct(s, f32) for s in shapes]
    out_specs = [vmem] * 3
    if last:
        out_shape = [jax.ShapeDtypeStruct((groups * BLK, heads * KVL), bf16)] + out_shape
        out_specs = [pl.BlockSpec(memory_space=pltpu.HBM)] + out_specs
    scratch = [
        pltpu.VMEM((PADDED // LANES, key_count, LANES), bf16),
        pltpu.VMEM((BLK, BLK), jnp.int32),
        pltpu.VMEM((rows, 2 * BLK), f32),
        pltpu.VMEM((rows, LANES), f32),
    ]
    if last:
        scratch += [pltpu.VMEM((groups, BLK, heads * KVL), bf16), pltpu.SemaphoreType.DMA((groups,))]
    at = 2 + len(pieces)
    result = pl.pallas_call(
        functools.partial(attend_kernel, layout, members, parts, chunk, where, units, unroll, last),
        out_shape=out_shape,
        in_specs=[pl.BlockSpec(memory_space=pltpu.SMEM)] + [vmem] * (1 + len(pieces) + len(state)),
        out_specs=out_specs,
        input_output_aliases={at + i: int(last) + i for i in range(len(state))},
        scratch_shapes=scratch,
        compiler_params=pltpu.CompilerParams(vmem_limit_bytes=LIMIT * 2**20),
        cost_estimate=pl.CostEstimate(flops=flops, bytes_accessed=1_000_000, transcendentals=0),
        name="attend",
    )(plan, q2, *pieces, *state)
    return result[0] if last else result


def per_device(n_pb, n_ka, tokens, kv_weight, queries, block_list):
    local_rows = tokens.shape[0]
    chunk = local_rows // n_pb
    key_count = local_rows * n_ka
    far = range(2, n_ka, 2)
    ring = [0] + list(far)
    phased = n_pb == 4 and chunk == UNIT

    def swap_core(piece, k):
        return swap(piece, "ka", 1, n_ka), [(d ^ 1, k) for d in ring]

    partials = project(tokens, kv_weight, n_pb)
    arrived = [partials[0]] + [swap(partials[k], "pb", k, n_pb) for k in range(1, n_pb)]
    first_row = lax.axis_index("ka") * local_rows + lax.axis_index("pb") * chunk
    phases, units = (3, (1, 1, 1)) if phased else (1, (2,))
    where = [item_base(phases, *block_list.shape, units, p) for p in range(phases)]
    plan = plan_items(block_list, phases, units)
    queries, plan, *arrived = lax.optimization_barrier((spread(queries), plan, *arrived))
    size = queries.shape[0], queries.shape[2]
    own = finish(arrived, first_row)
    spans = [swap(own, "ka", k, n_ka) for k in far]
    *state, spans[0] = lax.optimization_barrier((*clear(own, *size), spans[0]))
    column = jnp.concatenate([own] + spans, axis=0)

    if not phased:
        sets = [(column, [(d, 0) for d in ring])]
        sets += [(swap(column, "pb", k, n_pb), [(d, k) for d in ring]) for k in range(1, n_pb)]
        sets += [swap_core(piece, offsets[0][1]) for piece, offsets in sets]
        return attend(plan, where[0], 2, queries, sets, None, n_pb, chunk, key_count, state, True)

    beside = [swap(column, "pb", k, n_pb) for k in (1, 2)]
    half = len(ring) // 2
    cut = half * packed_rows(chunk)
    others = [(own, ring[:1]), (column[packed_rows(chunk) :], ring[1:])]
    others = [(swap(piece, "ka", 1, n_ka), [(d ^ 1, 0) for d in offsets]) for piece, offsets in others]
    sets = [(column, [(d, 0) for d in ring]), *others]
    state = attend(
        plan, where[0], 1, queries, sets, [0], n_pb, chunk, key_count // 4, state, False, flops=1_000_000
    )

    *state, x, y = lax.optimization_barrier((*state, *beside))
    other_x, other_y = swap_core(x, 1)[0], swap_core(y, 2)[0]
    sets = [(x, [(d, 1) for d in ring]), (y, [(d, 2) for d in ring])]
    sets += [(other_x, [(d ^ 1, 1) for d in ring]), (other_y, [(d ^ 1, 2) for d in ring])]
    near, far_half = pick(cut, x, y, other_x, other_y)
    corner = [
        (swap(near, "pb", 1, n_pb), [(d ^ core, 3) for core in (0, 1) for d in ring[:half]]),
        (swap(far_half, "pb", 2, n_pb), [(d ^ core, 3) for core in (0, 1) for d in ring[half:]]),
    ]
    state = attend(plan, where[1], 1, queries, sets, [1, 2], n_pb, chunk, key_count // 2, list(state), False, unroll=4)

    held = lax.optimization_barrier((*state, *[piece for piece, _ in corner]))
    state, corner = list(held[:3]), [(piece, offsets) for piece, (_, offsets) in zip(held[3:], corner)]
    return attend(plan, where[2], 1, queries, corner, [3], n_pb, chunk, key_count // 4, state, True)


def solution(mesh):
    in_specs = (P("ka", "pb"), P("pb", None), P("pb", "ka"), P("pb", None))
    out_specs = P("pb", "ka")
    return jax.shard_map(
        functools.partial(per_device, mesh.shape["pb"], mesh.shape["ka"]),
        mesh=mesh,
        in_specs=in_specs,
        out_specs=out_specs,
        check_vma=False,
    )
```

```python
import functools
import math

import jax
import jax.numpy as jnp
from jax import lax
from jax.experimental import pallas as pl
from jax.experimental.pallas import tpu as pltpu
from jax.sharding import PartitionSpec as P

KVL = 512
RD = 64
QK = 192
BLK = 128
LANES = 128
WIDTH = KVL + RD
PADDED = KVL + 2 * RD
MASKED = -1e30
LOWEST = -3e38
UNIT = BLK // 2
SENT = jnp.float32
TILE = 1024
SPREAD_LIMIT = 2
LIMIT = 20
SCALE = math.log2(math.e) / math.sqrt(QK)


def packed_rows(rows):
    return rows * 4 + (rows // 2 if rows % 32 == 0 else rows)


def swap(x, axis_name, offset, count):
    return lax.ppermute(x, axis_name, [(i, i ^ offset) for i in range(count)])


def project_kernel(cuts, tokens_ref, weight_ref, *rest):
    outs, (tok, wgt, total, sem) = rest[:-4], rest[-4:]
    copies = []
    for t, (start, depth) in enumerate(cuts):
        cut = pl.ds(start, depth)
        pair = [
            pltpu.make_async_copy(tokens_ref.at[:, cut], tok.at[:, cut], sem.at[0, t]),
            pltpu.make_async_copy(weight_ref.at[:, cut], wgt.at[:, cut], sem.at[1, t]),
        ]
        for copy in pair:
            copy.start()
        copies.append(pair)
    for t, (start, depth) in enumerate(cuts):
        for copy in copies[t]:
            copy.wait()
        cut = slice(start, start + depth)
        part = lax.dot_general(
            tok[:, cut], wgt[:, cut], (((1,), (1,)), ((), ())), preferred_element_type=jnp.float32
        )
        total[...] = part if t == 0 else total[...] + part
    rows = outs[0].shape[0]
    me = lax.axis_index("pb")
    for k, out in enumerate(outs):
        out[...] = total[pl.ds(pl.multiple_of((me ^ k) * rows, rows), rows), :].astype(out.dtype)


def project(tokens, kv_weight, parts):
    rows, features = tokens.shape
    depth = 896
    cuts = [(start, min(depth, features - start)) for start in range(0, features, depth)]
    return pl.pallas_call(
        functools.partial(project_kernel, cuts),
        out_shape=[jax.ShapeDtypeStruct((rows // parts, WIDTH), jnp.float32 if k == 0 else SENT) for k in range(parts)],
        in_specs=[pl.BlockSpec(memory_space=pltpu.HBM)] * 2,
        out_specs=[pl.BlockSpec(memory_space=pltpu.VMEM)] * parts,
        scratch_shapes=[
            pltpu.VMEM((rows, features), jnp.bfloat16),
            pltpu.VMEM((WIDTH, features), jnp.bfloat16),
            pltpu.VMEM((rows, WIDTH), jnp.float32),
            pltpu.SemaphoreType.DMA((2, len(cuts))),
        ],
        compiler_params=pltpu.CompilerParams(vmem_limit_bytes=60 * 2**20),
        name="project",
    )(tokens, kv_weight.T)


def finish_kernel(cos_ref, sin_ref, *rest):
    parts, out = rest[:-1], rest[-1]
    total = parts[0][...]
    for part in parts[1:]:
        total = total + part[...].astype(jnp.float32)
    rows = total.shape[0]
    latent = total[:, :KVL]
    latent = latent * lax.rsqrt(jnp.mean(latent * latent, axis=-1, keepdims=True) + 1e-06)
    for c in range(KVL // LANES):
        out[c * rows : (c + 1) * rows, :] = latent[:, c * LANES : (c + 1) * LANES].astype(jnp.bfloat16)
    rotary = total[:, KVL:]
    half = RD // 2
    turned = jnp.concatenate([rotary[:, half:], rotary[:, :half]], axis=1)
    rotary = rotary * cos_ref[...] + turned * sin_ref[...]
    if rows % 32 == 0:
        both = jnp.concatenate([rotary[: rows // 2], rotary[rows // 2 :]], axis=1)
    else:
        both = jnp.concatenate([rotary, jnp.zeros_like(rotary)], axis=1)
    out[4 * rows :, :] = both.astype(jnp.bfloat16)


def finish(parts, first_row):
    rows = parts[0].shape[0]
    half = RD // 2
    freq = jnp.exp(jnp.arange(half, dtype=jnp.float32) * (-2.0 * math.log(10000.0) / RD))
    position = (first_row + jnp.arange(rows, dtype=jnp.int32)).astype(jnp.float32)
    angle = position[:, None] * freq[None, :]
    cosine, sine = jnp.cos(angle), jnp.sin(angle)
    cosine = jnp.concatenate([cosine, cosine], axis=1)
    sine = jnp.concatenate([-sine, sine], axis=1)
    return pl.pallas_call(
        finish_kernel,
        out_shape=jax.ShapeDtypeStruct((packed_rows(rows), LANES), jnp.bfloat16),
        in_specs=[pl.BlockSpec(memory_space=pltpu.VMEM)] * (2 + len(parts)),
        out_specs=pl.BlockSpec(memory_space=pltpu.VMEM),
        compiler_params=pltpu.CompilerParams(vmem_limit_bytes=4 * 2**20),
        name="finish",
    )(cosine, sine, *parts)


def plan_kernel(phases, units, list_ref, plan_ref):
    groups, slots = list_ref.shape
    side = lax.axis_index("pb") // 2
    width = slots + 4
    base = entry_base(phases, groups, slots, units)
    counts = [[], [], []]
    for g in range(groups):
        at = [jnp.int32(0), jnp.int32(0), jnp.int32(0)]
        for t in range(slots):
            b = list_ref[g, t]
            live = (b >= 0).astype(jnp.int32)
            kind = (b & 1) ^ side
            plan_ref[base + g * width + t] = b
            for k in range(2):
                if phases > 1:
                    plan_ref[base + ((1 + k) * groups + g) * width + at[1 + k]] = b
                    at[1 + k] = at[1 + k] + jnp.where(kind == k, live, 0)
            at[0] = at[0] + live
        for k in range(3 if phases > 1 else 1):
            counts[k].append(at[k])
            for t in range(4):
                plan_ref[base + (k * groups + g) * width + at[k] + t] = -1
    for p in range(phases):
        kind = phase_kind(phases, p)
        step = 4 // units[p]
        where = item_base(phases, groups, slots, units, p)
        total = jnp.int32(0)
        for g in range(groups):
            n = (counts[kind][g] + step - 1) // step
            if p == phases - 1 or g == 0:
                n = jnp.maximum(n, 1)

            @pl.loop(0, n)
            def _(k, g=g, total=total):
                plan_ref[where + 1 + 2 * (total + k)] = g
                plan_ref[where + 2 + 2 * (total + k)] = base + (kind * groups + g) * width + k * step

            total = total + n
        plan_ref[where] = total


def phase_kind(phases, phase):
    return 0 if phases == 1 else (1, 0, 2)[phase]


def item_base(phases, groups, slots, units, phase):
    return sum(1 + 2 * (groups * (slots * u // 4 + 1) + 1) for u in units[:phase])


def entry_base(phases, groups, slots, units):
    return item_base(phases, groups, slots, units, phases)


def plan_items(block_list, phases, units):
    groups, slots = block_list.shape
    size = entry_base(phases, groups, slots, units) + (3 if phases > 1 else 1) * groups * (slots + 4)
    return pl.pallas_call(
        functools.partial(plan_kernel, phases, units),
        out_shape=jax.ShapeDtypeStruct((size,), jnp.int32),
        in_specs=[pl.BlockSpec(memory_space=pltpu.SMEM)],
        out_specs=pl.BlockSpec(memory_space=pltpu.SMEM),
        compiler_params=pltpu.CompilerParams(vmem_limit_bytes=2**20),
        name="plan",
    )(block_list)


def spread_kernel(q_ref, o_ref):
    width = q_ref.shape[1]
    for g in range(o_ref.shape[0]):
        rows = slice(g * BLK, (g + 1) * BLK)
        for h in range(width // WIDTH):
            c = h * WIDTH
            if c % LANES:
                part = q_ref[rows, c - RD : c + WIDTH]
                part = jnp.concatenate([part[:, RD:], part[:, :RD]], axis=1)
            elif c + PADDED <= width:
                part = q_ref[rows, c : c + PADDED]
            else:
                part = jnp.concatenate([q_ref[rows, c : c + WIDTH], jnp.zeros((BLK, RD), jnp.bfloat16)], axis=1)
            for c in range(PADDED // LANES):
                o_ref[g, c, h * BLK : (h + 1) * BLK, :] = part[:, c * LANES : (c + 1) * LANES]


def spread(queries):
    groups, heads = queries.shape[0] // BLK, queries.shape[1] // WIDTH
    vmem = pl.BlockSpec(memory_space=pltpu.VMEM)
    return pl.pallas_call(
        spread_kernel,
        in_specs=[vmem],
        out_specs=vmem,
        out_shape=jax.ShapeDtypeStruct((groups, PADDED // LANES, heads * BLK, LANES), jnp.bfloat16),
        compiler_params=pltpu.CompilerParams(vmem_limit_bytes=SPREAD_LIMIT * 2**20),
        cost_estimate=pl.CostEstimate(flops=0, bytes_accessed=10_000_000, transcendentals=0),
        name="spread",
    )(queries)


def pick_kernel(cut, x, y, other_x, other_y, near, far):
    near[:cut, :] = y[:cut, :]
    near[cut:, :] = other_y[:cut, :]
    far[: far.shape[0] // 2, :] = x[cut:, :]
    far[far.shape[0] // 2 :, :] = other_x[cut:, :]


def pick(cut, x, y, other_x, other_y):
    vmem = pl.BlockSpec(memory_space=pltpu.VMEM)
    return pl.pallas_call(
        functools.partial(pick_kernel, cut),
        out_shape=[
            jax.ShapeDtypeStruct((2 * cut, LANES), jnp.bfloat16),
            jax.ShapeDtypeStruct((2 * (x.shape[0] - cut), LANES), jnp.bfloat16),
        ],
        in_specs=[vmem] * 4,
        out_specs=[vmem] * 2,
        compiler_params=pltpu.CompilerParams(vmem_limit_bytes=2**20),
        name="pick",
    )(x, y, other_x, other_y)


def clear_kernel(ready_ref, m_ref, l_ref, acc):
    m_ref[...] = jnp.full_like(m_ref, LOWEST)
    l_ref[...] = jnp.zeros_like(l_ref)
    acc[...] = jnp.zeros_like(acc)


def clear(ready, groups, rows):
    shapes = [(groups, rows, LANES), (groups, rows, LANES), (groups, rows, KVL)]
    return pl.pallas_call(
        clear_kernel,
        out_shape=[jax.ShapeDtypeStruct(s, jnp.float32) for s in shapes],
        in_specs=[pl.BlockSpec(memory_space=pl.ANY)],
        out_specs=[pl.BlockSpec(memory_space=pltpu.VMEM)] * 3,
        compiler_params=pltpu.CompilerParams(vmem_limit_bytes=2**20),
        name="clear",
    )(ready)


def attend_kernel(layout, members, parts, chunk, where, units, unroll, last, plan_ref, q2, *refs):
    pieces, refs = refs[: len(layout)], list(refs[len(layout) :])
    refs = refs[3:]
    if last:
        out_hbm = refs.pop(0)
    m_ref, l_ref, acc = refs[:3]
    kx, gap, s_ref, p_ref = refs[3:7]
    if last:
        obuf, sem_o = refs[7:]
    groups, _, rows, _ = q2.shape
    heads = rows // BLK
    tile = min(TILE, rows)
    packed = packed_rows(chunk)
    pb, ka = lax.axis_index("pb"), lax.axis_index("ka")
    items = plan_ref[where]
    per_group = parts * chunk // UNIT

    row = lax.broadcasted_iota(jnp.int32, (BLK, BLK), 0)
    column = lax.broadcasted_iota(jnp.int32, (BLK, BLK), 1)
    gap[...] = row - column % UNIT
    kx[KVL // LANES] = jnp.zeros(kx.shape[1:], jnp.bfloat16)
    for piece, offsets in zip(pieces, layout):
        for at, (dk, dq) in enumerate(offsets):
            at *= packed
            if members is None:
                row = ((ka ^ dk) * parts + (pb ^ dq)) * chunk
            else:
                row = ((ka ^ dk) * len(members) + members.index(dq)) * chunk
            row = pl.multiple_of(row, chunk)
            for c in range(KVL // LANES):
                kx[c, pl.ds(row, chunk), :] = piece[at + c * chunk : at + (c + 1) * chunk, :]
            rotary = piece[at + 4 * chunk : at + packed, :]
            if chunk % 32 == 0:
                kx[KVL // LANES, pl.ds(row, chunk // 2), :RD] = rotary[:, :RD]
                kx[KVL // LANES, pl.ds(row + chunk // 2, chunk // 2), :RD] = rotary[:, RD:]
            else:
                kx[KVL // LANES, pl.ds(row, chunk), :] = rotary

    def group_of(t):
        return plan_ref[where + 1 + 2 * t]

    def key_units(t):
        entry = plan_ref[where + 2 + 2 * t]
        found = []
        for i in range(4):
            b = plan_ref[entry + i // units]
            known = jnp.maximum(b, 0)
            if members is None:
                unit = known * 2 + i % units
                row = unit
            else:
                index = jnp.int32(0)
                seat = pb ^ members[0]
                if len(members) == 2:
                    index = (known & 1) ^ (pb // 2)
                    seat = jnp.where(index == 0, seat, pb ^ members[1])
                unit = known * 2 + seat % 2
                row = known // (per_group // 2) * len(members) + index
            found.append((pl.multiple_of(row * UNIT, UNIT), jnp.where(b >= 0, unit * UNIT, 1 << 24)))
        return found

    def key_rows(found, width):
        columns = range(width // LANES)
        units = [jnp.concatenate([kx[c, pl.ds(row, UNIT), :] for c in columns], axis=1) for row, _ in found]
        return jnp.concatenate(units, axis=0)

    def mask(found, g):
        here = (pb * groups + g) * BLK
        left = lax.broadcasted_iota(jnp.int32, (BLK, BLK), 1) < UNIT
        bias = []
        for i in range(2):
            seen = [found[2 * i + k][1] - here for k in range(2)]
            bias.append(jnp.where(gap[...] >= jnp.where(left, seen[0], seen[1]), 0.0, MASKED))
        return bias

    def score(g, r, keys, bias):
        s = lax.dot_general(
            jnp.concatenate([q2[g, c, r : r + tile, :] for c in range(PADDED // LANES)], axis=1), keys, (((1,), (1,)), ((), ())), preferred_element_type=jnp.float32
        )
        for h in range(0, tile, BLK):
            sl = slice(r + h, r + h + BLK)
            s0 = s[h : h + BLK, :BLK] + bias[0]
            s1 = s[h : h + BLK, BLK:] + bias[1]
            s_ref[sl, :BLK] = s0
            s_ref[sl, BLK:] = s1
            p_ref[sl, :] = jnp.maximum(s0, s1)

    def weigh(g, r):
        weights, fades = [], []
        for h in range(0, tile, BLK):
            sl = slice(r + h, r + h + BLK)
            old = m_ref[g, sl, :]
            new = jnp.maximum(old, jnp.max(p_ref[sl, :], axis=1, keepdims=True) * SCALE)
            fade = jnp.exp2(old - new)
            e0 = jnp.exp2(s_ref[sl, :BLK] * SCALE - new)
            e1 = jnp.exp2(s_ref[sl, BLK:] * SCALE - new)
            m_ref[g, sl, :] = new
            l_ref[g, sl, :] = l_ref[g, sl, :] * fade + (e0 + e1)
            weights.append(jnp.concatenate([e0.astype(jnp.bfloat16), e1.astype(jnp.bfloat16)], axis=1))
            fades.append(fade)
        return jnp.concatenate(weights, axis=0), fades

    def blend(g, r, weights, fades, values):
        o = jnp.dot(weights, values, preferred_element_type=jnp.float32)
        for h in range(0, tile, BLK):
            sl = slice(r + h, r + h + BLK)
            for c in range(0, KVL, LANES):
                acc[g, sl, c : c + LANES] = (
                    acc[g, sl, c : c + LANES] * fades[h // BLK] + o[h : h + BLK, c : c + LANES]
                )

    def out_copy(g):
        rows_out = pl.ds(pl.multiple_of(g * BLK, BLK), BLK)
        return pltpu.make_async_copy(obuf.at[g], out_hbm.at[rows_out, :], sem_o.at[g])

    def end(g):
        for h in range(heads):
            sl = slice(h * BLK, (h + 1) * BLK)
            inverse = 1.0 / jnp.sum(l_ref[g, sl, :], axis=1, keepdims=True)
            obuf[g, :, h * KVL : (h + 1) * KVL] = (acc[g, sl, :] * inverse).astype(jnp.bfloat16)
        out_copy(g).start()

    def turn(t, g):
        @pl.when(group_of(t + 1) != g)
        def _():
            end(g)

    def ahead(t):
        found, g = key_units(t), group_of(t)
        keys, bias = key_rows(found, PADDED), mask(found, g)
        for r in range(0, rows, tile):
            score(g, r, keys, bias)

    def step(t, more):
        g = group_of(t)
        values = key_rows(key_units(t), KVL)
        parts_now = [weigh(g, r) for r in range(0, rows, tile)]
        if more:
            ahead(t + 1)
        for r, (weights, fades) in zip(range(0, rows, tile), parts_now):
            blend(g, r, weights, fades, values)

    turns = items - 1

    def steps(start, count):
        for k in range(count):
            step(start + k, True)
        if last:
            for k in range(count):
                turn(start + k, group_of(start + k))

    ahead(0)

    @pl.loop(0, turns // unroll)
    def _(i):
        steps(unroll * i, unroll)

    width = unroll
    while width > 1:
        width //= 2

        @pl.when((turns & width) != 0)
        def _(width=width):
            steps(turns // (2 * width) * (2 * width), width)

    step(turns, False)
    if last:
        end(group_of(turns))

    if last:
        for g in range(groups):
            out_copy(g).wait()


def attend(plan, where, units, q2, sets, members, parts, chunk, key_count, state, last, unroll=2, flops=5_000_000_000):
    pieces, layout = [piece for piece, _ in sets], [offsets for _, offsets in sets]
    groups, _, rows, _ = q2.shape
    heads = rows // BLK
    f32, bf16 = jnp.float32, jnp.bfloat16
    vmem = pl.BlockSpec(memory_space=pltpu.VMEM)
    shapes = [(groups, rows, LANES), (groups, rows, LANES), (groups, rows, KVL)]
    out_shape = [jax.ShapeDtypeStruct(s, f32) for s in shapes]
    out_specs = [vmem] * 3
    if last:
        out_shape = [jax.ShapeDtypeStruct((groups * BLK, heads * KVL), bf16)] + out_shape
        out_specs = [pl.BlockSpec(memory_space=pltpu.HBM)] + out_specs
    scratch = [
        pltpu.VMEM((PADDED // LANES, key_count, LANES), bf16),
        pltpu.VMEM((BLK, BLK), jnp.int32),
        pltpu.VMEM((rows, 2 * BLK), f32),
        pltpu.VMEM((rows, LANES), f32),
    ]
    if last:
        scratch += [pltpu.VMEM((groups, BLK, heads * KVL), bf16), pltpu.SemaphoreType.DMA((groups,))]
    at = 2 + len(pieces)
    result = pl.pallas_call(
        functools.partial(attend_kernel, layout, members, parts, chunk, where, units, unroll, last),
        out_shape=out_shape,
        in_specs=[pl.BlockSpec(memory_space=pltpu.SMEM)] + [vmem] * (1 + len(pieces) + len(state)),
        out_specs=out_specs,
        input_output_aliases={at + i: int(last) + i for i in range(len(state))},
        scratch_shapes=scratch,
        compiler_params=pltpu.CompilerParams(vmem_limit_bytes=LIMIT * 2**20),
        cost_estimate=pl.CostEstimate(flops=flops, bytes_accessed=1_000_000, transcendentals=0),
        name="attend",
    )(plan, q2, *pieces, *state)
    return result[0] if last else result


def per_device(n_pb, n_ka, tokens, kv_weight, queries, block_list):
    local_rows = tokens.shape[0]
    chunk = local_rows // n_pb
    key_count = local_rows * n_ka
    far = range(2, n_ka, 2)
    ring = [0] + list(far)
    phased = n_pb == 4 and chunk == UNIT

    def swap_core(piece, k):
        return swap(piece, "ka", 1, n_ka), [(d ^ 1, k) for d in ring]

    partials = project(tokens, kv_weight, n_pb)
    arrived = [partials[0]] + [swap(partials[k], "pb", k, n_pb) for k in range(1, n_pb)]
    first_row = lax.axis_index("ka") * local_rows + lax.axis_index("pb") * chunk
    phases, units = (3, (1, 1, 1)) if phased else (1, (2,))
    where = [item_base(phases, *block_list.shape, units, p) for p in range(phases)]
    plan = plan_items(block_list, phases, units)
    queries, plan, *arrived = lax.optimization_barrier((spread(queries), plan, *arrived))
    size = queries.shape[0], queries.shape[2]
    own = finish(arrived, first_row)
    spans = [swap(own, "ka", k, n_ka) for k in far]
    *state, spans[0] = lax.optimization_barrier((*clear(own, *size), spans[0]))
    column = jnp.concatenate([own] + spans, axis=0)

    if not phased:
        sets = [(column, [(d, 0) for d in ring])]
        sets += [(swap(column, "pb", k, n_pb), [(d, k) for d in ring]) for k in range(1, n_pb)]
        sets += [swap_core(piece, offsets[0][1]) for piece, offsets in sets]
        return attend(plan, where[0], 2, queries, sets, None, n_pb, chunk, key_count, state, True)

    beside = [swap(column, "pb", k, n_pb) for k in (1, 2)]
    half = len(ring) // 2
    cut = half * packed_rows(chunk)
    others = [(own, ring[:1]), (column[packed_rows(chunk) :], ring[1:])]
    others = [(swap(piece, "ka", 1, n_ka), [(d ^ 1, 0) for d in offsets]) for piece, offsets in others]
    sets = [(column, [(d, 0) for d in ring]), *others]
    state = attend(
        plan, where[0], 1, queries, sets, [0], n_pb, chunk, key_count // 4, state, False, unroll=4, flops=1_000_000
    )

    *state, x, y = lax.optimization_barrier((*state, *beside))
    other_x, other_y = swap_core(x, 1)[0], swap_core(y, 2)[0]
    sets = [(x, [(d, 1) for d in ring]), (y, [(d, 2) for d in ring])]
    sets += [(other_x, [(d ^ 1, 1) for d in ring]), (other_y, [(d ^ 1, 2) for d in ring])]
    near, far_half = pick(cut, x, y, other_x, other_y)
    corner = [
        (swap(near, "pb", 1, n_pb), [(d ^ core, 3) for core in (0, 1) for d in ring[:half]]),
        (swap(far_half, "pb", 2, n_pb), [(d ^ core, 3) for core in (0, 1) for d in ring[half:]]),
    ]
    state = attend(plan, where[1], 1, queries, sets, [1, 2], n_pb, chunk, key_count // 2, list(state), False, unroll=4)

    held = lax.optimization_barrier((*state, *[piece for piece, _ in corner]))
    state, corner = list(held[:3]), [(piece, offsets) for piece, (_, offsets) in zip(held[3:], corner)]
    return attend(plan, where[2], 1, queries, corner, [3], n_pb, chunk, key_count // 4, state, True)


def solution(mesh):
    in_specs = (P("ka", "pb"), P("pb", None), P("pb", "ka"), P("pb", None))
    out_specs = P("pb", "ka")
    return jax.shard_map(
        functools.partial(per_device, mesh.shape["pb"], mesh.shape["ka"]),
        mesh=mesh,
        in_specs=in_specs,
        out_specs=out_specs,
        check_vma=False,
    )
```
